512 devices in a mesh: task: 16 (over y, core), tile: 32 (over x, z).
Axes of the slice: x: 4, y: 8, z: 8, core: 2. Of those that a mesh axis runs over, the one named last changes fastest.
Arguments:
- deltas: bfloat16 [16, 4096, 16384], P('task', None, 'tile'), may hold values from -8 to 8
- sketches: bfloat16 [16, 16384, 16], P('task', 'tile'), may hold values from -6 to 6
Outputs:
- merged: bfloat16 [4096, 16384], P('task', 'tile')
The draws below stay inside these ranges and needn't reach their ends.
All inputs are finite; a program needn't handle non-finite values.
Results may differ from the reference program's by a relative error of at most 0.0025.
Values may be sent and summed in bfloat16 or wider, within the bound.
A program may use at most 64 MiB of HBM per device.

```python
import math
import jax
import jax.numpy as jnp
from jax import lax

D = 4096
F = 16384
K = 16
NEWTON = 5
TASKS = 16


def draw_deltas(key, part):
    key = jax.random.fold_in(key, 11)
    key_rows, key_cols, key_noise = jax.random.split(key, 3)
    row_signs = (jax.random.randint(key_rows, (TASKS, D, K), 0, 2) * 2 - 1).astype(jnp.float32)
    col_signs = (jax.random.randint(key_cols, (TASKS, F, K), 0, 2) * 2 - 1).astype(jnp.float32)
    strengths = (2 * K - jnp.arange(K)).astype(jnp.float32)
    signal = jnp.einsum('tdk,tfk->tdf', row_signs * strengths, col_signs)
    factor = 10.0 * (math.sqrt(D) + math.sqrt(F)) / (K * math.sqrt(D * F))
    noise = jnp.clip(jax.random.normal(key_noise, (TASKS, D, F), jnp.float32), -6.0, 6.0)
    return (0.5 * (factor * signal + noise)).astype(jnp.bfloat16)


def levels(stream_key, shape, shards, low, high):
    level, own = 1.0, jax.random.fold_in(stream_key, 6)
    for dim, parts in shards:
        heights = jnp.exp(jax.random.uniform(jax.random.fold_in(own, dim), (parts,), jnp.float32, low / len(shards), high / len(shards)))
        level = level * jnp.repeat(heights, shape[dim] // parts).reshape([-1 if axis == dim else 1 for axis in range(len(shape))])
    return level


def gaussian(rng, dims, width, most, cuts=(), kind=jnp.bfloat16):
    factor_of = levels(rng, dims, cuts, -0.22, 0.18) if cuts else 1.0
    result = jax.random.normal(rng, dims, jnp.float32) * width * factor_of
    return jnp.minimum(jnp.maximum(result, -most), most).astype(kind)


def setup_inputs(seed: int = 0) -> dict:
    keys = jax.random.split(jax.random.key(seed), 3)
    deltas = draw_deltas(jax.random.fold_in(keys[2], 71), 0)
    sketches = gaussian(keys[1], (TASKS, F, K), 1.0, 6.0, ((0, 16), (1, 32)))
    return {"deltas": deltas, "sketches": sketches}


HIGH = lax.Precision.HIGHEST

def column_gram(matrix):
    return lax.dot_general(matrix.astype(jnp.float32), matrix.astype(jnp.float32), (((0,), (0,)), ((), ())), precision=HIGH, preferred_element_type=jnp.float32)

def orthonormal(matrix):
    factor = jnp.linalg.cholesky(column_gram(matrix))
    basis = lax.linalg.triangular_solve(factor, matrix, left_side=False, lower=True, transpose_a=True)
    return (basis, factor)

def transposed_product(weights, basis):
    return lax.dot_general(weights.astype(jnp.float32), basis.astype(jnp.bfloat16).astype(jnp.float32), (((0,), (0,)), ((), ())), preferred_element_type=jnp.float32)

def factor_task(pair):
    weights, sketch = pair
    sketched = jnp.dot(weights.astype(jnp.float32), sketch.astype(jnp.float32), preferred_element_type=jnp.float32)
    first_basis, unused = orthonormal(sketched)
    power_basis, unused = orthonormal(transposed_product(weights, first_basis))
    left_basis, unused = orthonormal(jnp.dot(weights.astype(jnp.float32), power_basis.astype(jnp.bfloat16).astype(jnp.float32), preferred_element_type=jnp.float32))
    right_basis, lower_factor = orthonormal(transposed_product(weights, left_basis))
    return (left_basis, right_basis, lower_factor)

def block_core(lowers):
    count = lowers.shape[0]
    rank = lowers.shape[1]
    identity = jnp.eye(count, dtype=jnp.float32)
    blocks = identity[:, None, :, None] * lowers[:, :, None, :]
    return blocks.reshape(count * rank, count * rank)

def whitening(gram_matrix):
    scale = jnp.sqrt(jnp.sum(gram_matrix * gram_matrix))
    identity = jnp.eye(gram_matrix.shape[0], dtype=jnp.float32)
    approx = gram_matrix / scale
    inverse = identity
    for newton_step in range(NEWTON):
        middle = 0.5 * (3.0 * identity - jnp.dot(inverse, approx, precision=HIGH))
        approx = jnp.dot(approx, middle, precision=HIGH)
        inverse = jnp.dot(middle, inverse, precision=HIGH)
    return inverse / jnp.sqrt(scale)

def reference(deltas, sketches):
    lefts, rights, lowers = lax.map(factor_task, (deltas, sketches))
    stacked_left = jnp.transpose(lefts, (1, 0, 2)).reshape(D, TASKS * K)
    stacked_right = jnp.transpose(rights, (1, 0, 2)).reshape(F, TASKS * K)
    blocks = block_core(lowers)
    left_white = whitening(column_gram(stacked_left))
    right_white = whitening(column_gram(stacked_right))
    middle = jnp.dot(jnp.dot(left_white, blocks, precision=HIGH), right_white, precision=HIGH)
    scaled_left = jnp.dot(stacked_left, middle, precision=HIGH)
    merged = lax.dot_general(scaled_left.astype(jnp.float32), stacked_right.astype(jnp.float32), (((1,), (1,)), ((), ())), precision=HIGH, preferred_element_type=jnp.float32)
    return merged.astype(jnp.bfloat16)
```

```python
import functools

import jax
import jax.numpy as jnp
from jax import lax
from jax.experimental import pallas as pl
from jax.experimental.pallas import tpu as pltpu
from jax.sharding import PartitionSpec as P

NEWTON = 5
RANK = 16
LANES = 128
RING_Z = 8
CORES = 2
CHUNKS = 8
MESH = pl.DeviceIdType.MESH
HIGH = lax.Precision.HIGHEST
F32 = jnp.float32
BF16 = jnp.bfloat16

NN = (((1,), (0,)), ((), ()))
NT = (((1,), (1,)), ((), ()))
TN = (((0,), (0,)), ((), ()))

SEMS = ("a1", "a2", "gx", "gz", "c1", "c2", "t1y", "t1c", "pm", "la", "ey", "ec",
        "f1l", "f2l", "f3ly", "f3lc", "f1r", "f2r", "f3ry", "f3rc")
SEM = {name: index for index, name in enumerate(SEMS)}


def dot(a, b, dims=NN):
    return lax.dot_general(a, b, dims, preferred_element_type=F32)


def dot_high(a, b, dims=NN):
    return lax.dot_general(a, b, dims, precision=HIGH, preferred_element_type=F32)


def split(x):
    high = x.astype(BF16)
    return high, (x - high.astype(F32)).astype(BF16)


def dot_split(a, b, dims=NN):
    return dot(a[0], b[0], dims) + (dot(a[0], b[1], dims) + dot(a[1], b[0], dims))


def rsqrt(x):
    r = lax.rsqrt(x)
    return r * (1.5 - 0.5 * x * r * r)


def cholesky(columns):
    columns = list(columns)
    scales = []
    for k in range(RANK):
        scale = rsqrt(columns[k][k : k + 1, :])
        scales.append(scale)
        columns[k] = columns[k] * scale
        for i in range(k + 1, RANK):
            columns[i] = columns[i] - columns[k][i : i + 1, :] * columns[k]
    return columns, scales


def lane_columns(gram):
    return [jnp.broadcast_to(gram[:, i : i + 1], (RANK, LANES)) for i in range(RANK)]


def forward_solve(factor, tiles):
    columns, scales = factor
    row = lax.broadcasted_iota(jnp.int32, (RANK, LANES), 0)
    tiles = list(tiles)
    for k in range(RANK):
        below = jnp.where(row > k, columns[k], 0.0)
        at = row == k
        for n, tile in enumerate(tiles):
            solved = tile[k : k + 1, :] * scales[k]
            tiles[n] = jnp.where(at, jnp.broadcast_to(solved, tile.shape), tile - below * solved)
    return tiles


def to_tiles(matrix):
    return [matrix[:, n : n + LANES] for n in range(0, matrix.shape[1], LANES)]


def whitening(gram_matrix, eye):
    size = gram_matrix.shape[0]
    scale = jnp.sqrt(jnp.sum(gram_matrix * gram_matrix, keepdims=True))
    approx = gram_matrix / scale
    inverse = None
    for step in range(NEWTON):
        approx_halves = split(approx)
        if step == 0:
            product = approx
        else:
            inverse_halves = split(inverse)
            product = dot_split(inverse_halves, approx_halves)
        middle = 0.5 * (3.0 * eye - product)
        middle_halves = split(middle)
        if step < NEWTON - 1:
            approx = dot_split(approx_halves, middle_halves)
        inverse = middle if step == 0 else dot_split(middle_halves, inverse_halves)
    return inverse / jnp.sqrt(scale)


def block_factors(gram_left, gram_right, size):
    tasks = size // RANK
    group = LANES // (2 * tasks)
    lane = lax.broadcasted_iota(jnp.int32, (RANK, size), 1)
    sub = lax.broadcasted_iota(jnp.int32, (RANK, size), 0)
    pick = lane % RANK == sub
    grams = (gram_left, gram_right)
    spread_row = lax.broadcasted_iota(jnp.int32, (size, LANES), 0) // RANK
    spread_lane = lax.broadcasted_iota(jnp.int32, (size, LANES), 1) // group
    total = None
    for side, gram in enumerate(grams):
        diagonal = jnp.zeros((RANK, size), F32)
        for b in range(tasks):
            diagonal = jnp.where(lane // RANK == b, gram[b * RANK : (b + 1) * RANK, :], diagonal)
        rows = [jnp.where(pick, jnp.broadcast_to(diagonal[i : i + 1, :], (RANK, size)), 0.0) for i in range(RANK)]
        stack = jnp.concatenate(rows, axis=0)
        spread = (spread_lane == spread_row + side * tasks).astype(F32)
        term = dot_high(stack, spread)
        total = term if total is None else total + term
    columns, scales = cholesky([total[i * RANK : (i + 1) * RANK, :] for i in range(RANK)])
    row = lax.broadcasted_iota(jnp.int32, (RANK, LANES), 0)
    inverse = [(row == i).astype(F32) for i in range(RANK)]
    for k in range(RANK):
        inverse[k] = inverse[k] * scales[k]
        for i in range(k + 1, RANK):
            inverse[i] = inverse[i] - columns[k][i : i + 1, :] * inverse[k]
    stack = jnp.concatenate(inverse, axis=0)
    back_lane = lax.broadcasted_iota(jnp.int32, (LANES, size), 0)
    back_col = lax.broadcasted_iota(jnp.int32, (LANES, size), 1) // RANK
    factors = []
    for side in range(2):
        back = (back_lane == (back_col + side * tasks) * group).astype(F32)
        wide = dot_high(stack, back)
        rows = [
            jnp.sum(jnp.where(pick, wide[i * RANK : (i + 1) * RANK, :], 0.0), axis=0, keepdims=True) for i in range(RANK)
        ]
        compact = jnp.concatenate(rows, axis=0)
        factors.append(jnp.concatenate([jnp.where(lane // RANK == b, compact, 0.0) for b in range(tasks)], axis=0))
    return factors


def kernel(tasks, tiles, d_hbm, sk_ref, out_ref, dv, a1s, a1r, a2, gxs, gxr, gzs, gzr, c1s, c1r, c2,
           sl, t1, la, e, f1ls, f1lr, f2l, f3l, f1rs, f1rr, f2r, f3r, load_sem, send_sem, recv_sem):
    me_t, me_j = lax.axis_index("task"), lax.axis_index("tile")
    ring_x = tiles // RING_Z
    ring_y = tasks // CORES
    x, z = me_j // RING_Z, me_j % RING_Z
    y, core = me_t // CORES, me_t % CORES
    rows = dv.shape[0]
    width = dv.shape[1]
    size = tasks * RANK
    per_task = tiles // tasks
    chunk = rows // CHUNKS

    loads = [
        pltpu.make_async_copy(
            d_hbm.at[0, pl.ds(n * chunk, chunk)], dv.at[pl.ds(n * chunk, chunk)], load_sem.at[n]
        )
        for n in range(CHUNKS)
    ]
    for load in loads:
        load.start()

    def tile_peer(k):
        return ((x + k // RING_Z) % ring_x) * RING_Z + (z + k % RING_Z) % RING_Z

    partner_t = me_j // per_task
    partner_j = me_t * per_task + me_j % per_task
    alone = partner_t == me_t
    twin = y * CORES + (1 - core)

    barrier = pltpu.get_barrier_semaphore()

    def greet(t, j):
        pl.semaphore_signal(barrier, inc=1, device_id=(t, j), device_id_type=MESH)

    def greet_tile(k, carry):
        greet(me_t, tile_peer(k))
        return carry

    def greet_y(k, carry):
        greet(((y + k) % ring_y) * CORES + core, me_j)
        return carry

    lax.fori_loop(1, tiles, greet_tile, 0)
    lax.fori_loop(1, ring_y, greet_y, 0)
    greet(twin, me_j)

    @pl.when(jnp.logical_not(alone))
    def _():
        greet(partner_t, partner_j)

    def send(src, dst, name, t, j):
        pltpu.make_async_remote_copy(
            src_ref=src, dst_ref=dst, send_sem=send_sem.at[SEM[name]], recv_sem=recv_sem.at[SEM[name]],
            device_id=(t, j), device_id_type=MESH,
        ).start()

    def wait(ref, count, sems, name):
        pltpu.make_async_copy(ref.at[pl.ds(0, count)], ref.at[pl.ds(0, count)], sems.at[SEM[name]]).wait()

    def to_tile(name, src, dst):
        def body(k, carry):
            j = tile_peer(k)
            send(src(j), dst(k), name, me_t, j)
            return carry

        lax.fori_loop(1, tiles, body, 0)

    def to_x(name, src, dst):
        def body(k, carry):
            send(src, dst.at[k], name, me_t, ((x + k) % ring_x) * RING_Z + z)
            return carry

        lax.fori_loop(1, ring_x, body, 0)

    def to_z(name, src, dst):
        def body(k, carry):
            send(src, dst.at[k], name, me_t, x * RING_Z + (z + k) % RING_Z)
            return carry

        lax.fori_loop(1, RING_Z, body, 0)

    def to_task(name, buf):
        send(buf.at[me_t], buf.at[me_t], name + "c", twin, me_j)

        def body(k, carry):
            send(buf.at[me_t], buf.at[me_t], name + "y", ((y + k) % ring_y) * CORES + core, me_j)
            return carry

        lax.fori_loop(1, ring_y, body, 0)

    def pass_on(name, buf):
        wait(buf, ring_y - 1, recv_sem, name + "y")

        def body(k, carry):
            t = ((y + k) % ring_y) * CORES + core
            send(buf.at[t], buf.at[t], name + "c", twin, me_j)
            return carry

        lax.fori_loop(1, ring_y, body, 0)

    sketch = sk_ref[0].astype(F32).T.astype(BF16)
    for n in range(CHUNKS):
        loads[n].wait()
        part = dot(sketch, dv[n * chunk : (n + 1) * chunk, :], NT).astype(BF16)
        for m in range(chunk // LANES):
            a1s[n * (chunk // LANES) + m] = part[:, m * LANES : (m + 1) * LANES]

    greeted = tiles - 1 + ring_y - 1 + 1 + jnp.where(alone, 0, 1)
    pl.semaphore_wait(barrier, greeted)

    to_tile("a1", lambda j: a1s.at[j], lambda k: a1r.at[k])
    wait(a1r, tiles - 1, recv_sem, "a1")
    total = a1s[me_j].astype(F32)
    for k in range(1, tiles):
        total += a1r[k].astype(F32)
    a2[me_j] = total.astype(BF16)
    to_tile("a2", lambda j: a2.at[me_j], lambda k: a2.at[me_j])
    wait(a2, tiles - 1, recv_sem, "a2")

    def project(blocks):
        basis = jnp.concatenate([blocks[j] for j in range(tiles)], axis=1)
        gram = dot(basis, basis, NT)
        product = jnp.zeros((RANK, width), F32)
        for n in range(CHUNKS):
            product += dot(basis[:, n * chunk : (n + 1) * chunk], dv[n * chunk : (n + 1) * chunk, :])
        factor = cholesky(lane_columns(gram))
        return jnp.concatenate(forward_solve(factor, to_tiles(product)), axis=1)

    power = project(a2)
    gram = dot_high(power, power, NT)
    gxs[...] = jnp.concatenate([gram, jnp.zeros((RANK, LANES - RANK), F32)], axis=1)
    to_x("gx", gxs, gxr)

    power_1 = power.astype(BF16)
    rest = power - power_1.astype(F32)
    power_2 = rest.astype(BF16)
    power_3 = (rest - power_2.astype(F32)).astype(BF16)
    parts = jnp.concatenate([power_1, power_2, power_3], axis=0)
    for n in range(CHUNKS):
        part = dot(parts, dv[n * chunk : (n + 1) * chunk, :], NT)
        part = part[:RANK] + (part[RANK : 2 * RANK] + part[2 * RANK :])
        for m in range(chunk // LANES):
            c1s[n * (chunk // LANES) + m] = part[:, m * LANES : (m + 1) * LANES]
    to_tile("c1", lambda j: c1s.at[j], lambda k: c1r.at[k])

    wait(gxr, ring_x - 1, recv_sem, "gx")
    total = gxs[...]
    for k in range(1, ring_x):
        total += gxr[k]
    gzs[...] = total
    to_z("gz", gzs, gzr)
    wait(gzr, RING_Z - 1, recv_sem, "gz")
    for k in range(1, RING_Z):
        total += gzr[k]
    power_factor = cholesky(lane_columns(total))

    wait(c1r, tiles - 1, recv_sem, "c1")
    total = c1s[me_j]
    for k in range(1, tiles):
        total += c1r[k]
    (left_slice,) = forward_solve(power_factor, [total])
    c2[me_j] = left_slice.astype(BF16)
    to_tile("c2", lambda j: c2.at[me_j], lambda k: c2.at[me_j])
    t1[me_t] = left_slice
    to_task("t1", t1)

    @pl.when(jnp.logical_not(alone))
    def _():
        sl[...] = left_slice
        send(sl, la.at[partner_j], "pm", partner_t, partner_j)

    @pl.when(alone)
    def _():
        la[me_j] = left_slice

    wait(c2, tiles - 1, recv_sem, "c2")
    e[me_t] = project(c2)
    to_task("e", e)

    @pl.when(jnp.logical_not(alone))
    def _():
        wait(la, 1, recv_sem, "pm")

    to_tile("la", lambda j: la.at[me_j], lambda k: la.at[me_j])

    def rows_out(block, buf):
        for h in range(size // LANES):
            for r in range(RANK):
                buf[h * RANK + r] = block[r : r + 1, h * LANES : (h + 1) * LANES]

    def reduced(name, own, received, gathered):
        wait(received, tiles - 1, recv_sem, name)
        total = own[me_j]
        for k in range(1, tiles):
            total += received[k]
        gathered[me_j] = total

    def block_row(gathered):
        return jnp.concatenate(
            [
                jnp.concatenate([gathered[h * RANK + r] for r in range(RANK)], axis=0)
                for h in range(size // LANES)
            ],
            axis=1,
        )

    pass_on("t1", t1)
    wait(t1, ring_y, recv_sem, "t1c")
    stacked = jnp.concatenate([t1[t] for t in range(tasks)], axis=0)
    rows_out(dot_high(t1[me_t], stacked, NT), f1ls)
    to_tile("f1l", lambda j: f1ls.at[j], lambda k: f1lr.at[k])

    pass_on("e", e)
    wait(e, ring_y, recv_sem, "ec")
    stacked = jnp.concatenate([e[t] for t in range(tasks)], axis=0)
    rows_out(dot_high(e[me_t], stacked, NT), f1rs)
    to_tile("f1r", lambda j: f1rs.at[j], lambda k: f1rr.at[k])

    reduced("f1l", f1ls, f1lr, f2l)
    to_tile("f2l", lambda j: f2l.at[me_j], lambda k: f2l.at[me_j])
    reduced("f1r", f1rs, f1rr, f2r)
    to_tile("f2r", lambda j: f2r.at[me_j], lambda k: f2r.at[me_j])

    wait(f2l, tiles - 1, recv_sem, "f2l")
    f3l[me_t] = block_row(f2l)
    to_task("f3l", f3l)
    wait(f2r, tiles - 1, recv_sem, "f2r")
    f3r[me_t] = block_row(f2r)
    to_task("f3r", f3r)
    pass_on("f3l", f3l)
    pass_on("f3r", f3r)
    wait(f3l, ring_y, recv_sem, "f3lc")
    wait(f3r, ring_y, recv_sem, "f3rc")

    gram_left = jnp.concatenate([f3l[t] for t in range(tasks)], axis=0)
    gram_right = jnp.concatenate([f3r[t] for t in range(tasks)], axis=0)
    row = lax.broadcasted_iota(jnp.int32, (size, size), 0)
    column = lax.broadcasted_iota(jnp.int32, (size, size), 1)
    eye = (row == column).astype(F32)
    left_inverse, right_inverse = block_factors(gram_left, gram_right, size)
    left_halves, right_halves = split(left_inverse), split(right_inverse)
    cores = jnp.where(row // RANK == column // RANK, gram_right, 0.0)
    cores = dot_split(split(cores), right_halves, NT)
    gram_left = dot_split(split(dot_split(left_halves, split(gram_left))), left_halves, NT)
    gram_right = dot_split(split(dot_split(right_halves, split(gram_right))), right_halves, NT)
    left_white = whitening(gram_left, eye)
    right_white = whitening(gram_right, eye)
    middle = dot_split(split(dot_split(split(left_white), split(cores))), split(right_white))

    wait(la, tiles - 1, recv_sem, "la")
    left_rows = jnp.concatenate(
        [
            jnp.concatenate([la[t * per_task + b] for b in range(per_task)], axis=1)
            for t in range(tasks)
        ],
        axis=0,
    )
    right = dot_split(right_halves, split(stacked))
    left = dot_split(left_halves, split(left_rows))
    scaled = dot_split(split(left), split(middle), TN)
    out_ref[...] = dot_split(split(scaled), split(right)).astype(BF16)

    for name, ref, count in (
        ("a1", a1s, tiles - 1), ("a2", a2, tiles - 1), ("gx", gxr, ring_x - 1), ("gz", gzr, RING_Z - 1),
        ("c1", c1s, tiles - 1), ("c2", c2, tiles - 1), ("t1y", t1, ring_y - 1), ("t1c", t1, ring_y),
        ("la", la, tiles - 1), ("ey", e, ring_y - 1), ("ec", e, ring_y),
        ("f1l", f1ls, tiles - 1), ("f2l", f2l, tiles - 1), ("f3ly", f3l, ring_y - 1), ("f3lc", f3l, ring_y),
        ("f1r", f1rs, tiles - 1), ("f2r", f2r, tiles - 1), ("f3ry", f3r, ring_y - 1), ("f3rc", f3r, ring_y),
    ):
        wait(ref, count, send_sem, name)

    @pl.when(jnp.logical_not(alone))
    def _():
        wait(la, 1, send_sem, "pm")


def on_device(tasks, tiles, deltas, sketches):
    rows, width = deltas.shape[1:]
    size = tasks * RANK
    pieces = (tiles, 1, LANES)
    block = (tiles, RANK, LANES)
    ring_x = tiles // RING_Z
    return pl.pallas_call(
        functools.partial(kernel, tasks, tiles),
        out_shape=jax.ShapeDtypeStruct((rows // tasks, width), BF16),
        in_specs=[pl.BlockSpec(memory_space=pl.ANY), pl.BlockSpec(memory_space=pltpu.VMEM)],
        out_specs=pl.BlockSpec(memory_space=pltpu.VMEM),
        scratch_shapes=[
            pltpu.VMEM((rows, width), BF16),
            pltpu.VMEM(block, BF16), pltpu.VMEM(block, BF16), pltpu.VMEM(block, BF16),
            pltpu.VMEM((RANK, LANES), F32), pltpu.VMEM((ring_x, RANK, LANES), F32),
            pltpu.VMEM((RANK, LANES), F32), pltpu.VMEM((RING_Z, RANK, LANES), F32),
            pltpu.VMEM(block, F32), pltpu.VMEM(block, F32), pltpu.VMEM(block, BF16),
            pltpu.VMEM((RANK, LANES), F32), pltpu.VMEM((tasks, RANK, LANES), F32), pltpu.VMEM(block, F32),
            pltpu.VMEM((tasks, RANK, width), F32),
            pltpu.VMEM(pieces, F32), pltpu.VMEM(pieces, F32), pltpu.VMEM(pieces, F32),
            pltpu.VMEM((tasks, RANK, size), F32),
            pltpu.VMEM(pieces, F32), pltpu.VMEM(pieces, F32), pltpu.VMEM(pieces, F32),
            pltpu.VMEM((tasks, RANK, size), F32),
            pltpu.SemaphoreType.DMA((CHUNKS,)),
            pltpu.SemaphoreType.DMA((len(SEMS),)),
            pltpu.SemaphoreType.DMA((len(SEMS),)),
        ],
        compiler_params=pltpu.CompilerParams(
            collective_id=0, has_side_effects=True, vmem_limit_bytes=48 * 2**20
        ),
    )(deltas, sketches)


def solution(mesh):
    tasks, tiles = mesh.shape["task"], mesh.shape["tile"]
    return jax.shard_map(
        functools.partial(on_device, tasks, tiles),
        mesh=mesh,
        in_specs=(P("task", None, "tile"), P("task", "tile", None)),
        out_specs=P("task", "tile"),
        check_vma=False,
    )
```

```python
import functools

import jax
import jax.numpy as jnp
from jax import lax
from jax.experimental import pallas as pl
from jax.experimental.pallas import tpu as pltpu
from jax.sharding import PartitionSpec as P

NEWTON = 5
RANK = 16
LANES = 128
RING_X, RING_Z = 4, 8
RING_Y, CORES = 8, 2
CHUNKS = 8
MESH = pl.DeviceIdType.MESH
HIGH = lax.Precision.HIGHEST
F32 = jnp.float32
BF16 = jnp.bfloat16

NN = (((1,), (0,)), ((), ()))
NT = (((1,), (1,)), ((), ()))
TN = (((0,), (0,)), ((), ()))

SEMS = ("a1", "a2", "gp", "c1", "c1x", "c2", "gl", "t1y", "t1c", "pm", "la", "ey", "ec", "ely", "elc", "gr",
        "dl", "dr", "rl", "al", "rr", "ar")
SEM = {name: index for index, name in enumerate(SEMS)}


def around(step, ring):
    return min(step, ring - step)


TILE_STEPS = sorted(
    ((a, b) for a in range(RING_X) for b in range(RING_Z) if (a, b) != (0, 0)),
    key=lambda step: -around(step[0], RING_X) - around(step[1], RING_Z),
)
Y_STEPS = sorted(range(1, RING_Y), key=lambda step: -around(step, RING_Y))


def dot(a, b, dims=NN):
    return lax.dot_general(a, b, dims, preferred_element_type=F32)


def dot_high(a, b, dims=NN):
    return lax.dot_general(a, b, dims, precision=HIGH, preferred_element_type=F32)


def split(x):
    high = x.astype(BF16)
    return high, (x - high.astype(F32)).astype(BF16)


def dot_split(a, b, dims=NN):
    return dot(a[0], b[0], dims) + (dot(a[0], b[1], dims) + dot(a[1], b[0], dims))


def rsqrt(x):
    r = lax.rsqrt(x)
    return r * (1.5 - 0.5 * x * r * r)


def cholesky(columns):
    columns = list(columns)
    scales = []
    for k in range(RANK):
        scale = rsqrt(columns[k][k : k + 1, :])
        scales.append(scale)
        columns[k] = columns[k] * scale
        for i in range(k + 1, RANK):
            columns[i] = columns[i] - columns[k][i : i + 1, :] * columns[k]
    return columns, scales


def lane_columns(gram):
    return [jnp.broadcast_to(gram[:, i : i + 1], (RANK, LANES)) for i in range(RANK)]


def forward_solve(factor, tiles):
    columns, scales = factor
    row = rows_of((RANK, LANES))
    tiles = list(tiles)
    for k in range(RANK):
        below = jnp.where(row > k, columns[k], 0.0)
        at = row == k
        for n, tile in enumerate(tiles):
            solved = tile[k : k + 1, :] * scales[k]
            tiles[n] = jnp.where(at, jnp.broadcast_to(solved, tile.shape), tile - below * solved)
    return tiles


def to_tiles(matrix):
    return [matrix[:, n : n + LANES] for n in range(0, matrix.shape[1], LANES)]


def whitening(gram_matrix, eye):
    size = gram_matrix.shape[0]
    scale = jnp.sqrt(jnp.sum(gram_matrix * gram_matrix, keepdims=True))
    approx = gram_matrix / scale
    inverse = None
    for step in range(NEWTON):
        approx_halves = split(approx)
        if step == 0:
            product = approx
        else:
            inverse_halves = split(inverse)
            product = dot_split(inverse_halves, approx_halves)
        middle = 0.5 * (3.0 * eye - product)
        middle_halves = split(middle)
        if step < NEWTON - 1:
            approx = dot_split(approx_halves, middle_halves)
        inverse = middle if step == 0 else dot_split(middle_halves, inverse_halves)
    return inverse / jnp.sqrt(scale)


def lanes_of(shape):
    return lax.broadcasted_iota(jnp.int32, shape, 1)


def rows_of(shape):
    return lax.broadcasted_iota(jnp.int32, shape, 0)


def repeat_lanes(wide):
    for shift in (RANK, 2 * RANK, 4 * RANK):
        wide = wide + pltpu.roll(wide, shift, 1)
    return wide


def pack(gram):
    shape = (RANK, LANES)
    wide = repeat_lanes(jnp.concatenate([gram, jnp.zeros((RANK, LANES - RANK), F32)], axis=1))
    wide = jnp.where(lanes_of(shape) // RANK == rows_of(shape) % 8, wide, 0.0)
    return jnp.concatenate(
        [jnp.sum(wide[:8], axis=0, keepdims=True), jnp.sum(wide[8:], axis=0, keepdims=True)], axis=0
    )


def unpack(packed):
    shape = (RANK, LANES)
    wide = jnp.where(rows_of(shape) < 8, packed[0:1, :], packed[1:2, :])
    return repeat_lanes(jnp.where(lanes_of(shape) // RANK == rows_of(shape) % 8, wide, 0.0))


def side_by_side(packed):
    shape = (RANK, LANES)
    halves = []
    for h in range(2):
        half = jnp.zeros(shape, F32)
        for b in range(8):
            half = jnp.where(lanes_of(shape) // RANK == b, unpack(packed[8 * h + b]), half)
        halves.append(half)
    return jnp.concatenate(halves, axis=1)


def block_diagonal(blocks):
    tasks = blocks.shape[1] // RANK
    lane = lanes_of(blocks.shape)
    return jnp.concatenate([jnp.where(lane // RANK == b, blocks, 0.0) for b in range(tasks)], axis=0)


def fold(gram):
    shape = (LANES, LANES)
    first = jnp.where(rows_of(shape) >= lanes_of(shape), gram[:LANES, :LANES], gram[LANES:, LANES:])
    return jnp.concatenate([first, gram[:LANES, LANES:]], axis=0)


def unfold(folded, blocks):
    shape = (LANES, LANES)
    first, cross = folded[:LANES], folded[LANES:]
    turned = first.T
    lower = rows_of(shape) >= lanes_of(shape)
    top = jnp.concatenate([jnp.where(lower, first, turned), cross], axis=1)
    bottom = jnp.concatenate([cross.T, jnp.where(lower, turned, first)], axis=1)
    gram = jnp.concatenate([top, bottom], axis=0)
    return jnp.where(rows_of(gram.shape) // RANK == lanes_of(gram.shape) // RANK, blocks, gram)


def three(x):
    first = x.astype(BF16)
    rest = x - first.astype(F32)
    second = rest.astype(BF16)
    return first, second, (rest - second.astype(F32)).astype(BF16)


def dot_ones(a, ones):
    first, second, third = three(a)
    return dot(first, ones) + (dot(second, ones) + dot(third, ones))


def block_factors(sides):
    size = sides[0].shape[1]
    tasks = size // RANK
    group = LANES // (2 * tasks)
    lane, sub = lanes_of((RANK, size)), rows_of((RANK, size))
    pick = lane % RANK == sub
    spread_row = rows_of((size, LANES)) // RANK
    spread_lane = lanes_of((size, LANES)) // group
    total = None
    for side, blocks in enumerate(sides):
        rows = [jnp.where(pick, jnp.broadcast_to(blocks[i : i + 1, :], (RANK, size)), 0.0) for i in range(RANK)]
        spread = (spread_lane == spread_row + side * tasks).astype(F32).astype(BF16)
        term = dot_ones(jnp.concatenate(rows, axis=0), spread)
        total = term if total is None else total + term
    columns, scales = cholesky([total[i * RANK : (i + 1) * RANK, :] for i in range(RANK)])
    row = rows_of((RANK, LANES))
    inverse = [(row == i).astype(F32) for i in range(RANK)]
    for k in range(RANK):
        inverse[k] = inverse[k] * scales[k]
        for i in range(k + 1, RANK):
            inverse[i] = inverse[i] - columns[k][i : i + 1, :] * inverse[k]
    stack = jnp.concatenate(inverse, axis=0)
    back_lane = rows_of((LANES, size))
    back_col = lanes_of((LANES, size)) // RANK
    factors = []
    for side in range(2):
        back = (back_lane == (back_col + side * tasks) * group).astype(F32).astype(BF16)
        wide = dot_ones(stack, back)
        rows = [
            jnp.sum(jnp.where(pick, wide[i * RANK : (i + 1) * RANK, :], 0.0), axis=0, keepdims=True) for i in range(RANK)
        ]
        factors.append(block_diagonal(jnp.concatenate(rows, axis=0)))
    return factors


def kernel(d_hbm, sk_hbm, out_ref, dv, skv, a1s, a1r, a2, gps, gpr, c1s, c1r, c1xs, c1xr, c2,
           gls, glr, grs, grr, dl, dr, sl, t1, la, eh, el, wls, wlr, wlg, wrs, wrr, wrg,
           load_sem, send_sem, recv_sem):
    me_t, me_j = lax.axis_index("task"), lax.axis_index("tile")
    x, z = me_j // RING_Z, me_j % RING_Z
    y, core = me_t // CORES, me_t % CORES
    rows, width = dv.shape
    tiles, tasks = la.shape[0], t1.shape[0]
    per_task = tiles // tasks
    chunk = rows // CHUNKS

    sketch_load = pltpu.make_async_copy(sk_hbm.at[0], skv, load_sem.at[CHUNKS])
    sketch_load.start()
    loads = [
        pltpu.make_async_copy(
            d_hbm.at[0, pl.ds(n * chunk, chunk)], dv.at[pl.ds(n * chunk, chunk)], load_sem.at[n]
        )
        for n in range(CHUNKS)
    ]
    for load in loads:
        load.start()

    xs = [((x + a) % RING_X) * RING_Z for a in range(RING_X)]
    zs = [(z + b) % RING_Z for b in range(RING_Z)]
    ys = [((y + c) % RING_Y) * CORES for c in range(RING_Y)]
    twin = y * CORES + (1 - core)
    partner_t = me_j // per_task
    partner_j = me_t * per_task + me_j % per_task
    alone = partner_t == me_t

    barrier = pltpu.get_barrier_semaphore()

    def greet(t, j):
        pl.semaphore_signal(barrier, inc=1, device_id=(t, j), device_id_type=MESH)

    for a, b in TILE_STEPS:
        greet(me_t, xs[a] + zs[b])
    for c in Y_STEPS:
        greet(ys[c] + core, me_j)
        greet(ys[c] + (1 - core), me_j)
    greet(twin, me_j)

    @pl.when(jnp.logical_not(alone))
    def _():
        greet(partner_t, partner_j)

    def send(src, dst, name, t, j):
        pltpu.make_async_remote_copy(
            src_ref=src, dst_ref=dst, send_sem=send_sem.at[SEM[name]], recv_sem=recv_sem.at[SEM[name]],
            device_id=(t, j), device_id_type=MESH,
        ).start()

    def wait(ref, count, sems, name):
        pltpu.make_async_copy(ref.at[pl.ds(0, count)], ref.at[pl.ds(0, count)], sems.at[SEM[name]]).wait()

    def scatter(name, src, dst):
        for a, b in TILE_STEPS:
            j = xs[a] + zs[b]
            send(src.at[j], dst.at[a * RING_Z + b], name, me_t, j)

    def to_each(name, src, dst):
        for a, b in TILE_STEPS:
            send(src, dst.at[a * RING_Z + b], name, me_t, xs[a] + zs[b])

    def gather(name, buf):
        for a, b in TILE_STEPS:
            send(buf.at[me_j], buf.at[me_j], name, me_t, xs[a] + zs[b])

    def received(name, own, buf):
        wait(buf, tiles - 1, recv_sem, name)
        total = own.astype(F32)
        for k in range(1, tiles):
            total += buf[k].astype(F32)
        return total

    def to_task(name, buf):
        for c in Y_STEPS:
            send(buf.at[me_t], buf.at[me_t], name + "y", ys[c] + core, me_j)
        send(buf.at[me_t], buf.at[me_t], name + "c", twin, me_j)

    def pass_on(name, buf):
        wait(buf, RING_Y - 1, recv_sem, name + "y")
        for c in Y_STEPS:
            t = ys[c] + core
            send(buf.at[t], buf.at[t], name + "c", twin, me_j)

    def to_task_direct(name, buf):
        for c in Y_STEPS:
            send(buf.at[me_t], buf.at[me_t], name, ys[c] + core, me_j)
            send(buf.at[me_t], buf.at[me_t], name, ys[c] + (1 - core), me_j)
        send(buf.at[me_t], buf.at[me_t], name, twin, me_j)

    def store_pieces(buf, matrix):
        for p in range(tiles):
            buf[p] = matrix[8 * p : 8 * p + 8, :]

    def pieces(buf):
        return jnp.concatenate([buf[p] for p in range(tiles)], axis=0)

    sketch_load.wait()
    sketch = skv[...]
    for n in range(CHUNKS):
        loads[n].wait()
        part = dot(sketch, dv[n * chunk : (n + 1) * chunk, :], NT).astype(BF16)
        for m in range(chunk // LANES):
            a1s[n * (chunk // LANES) + m] = part[:, m * LANES : (m + 1) * LANES]

    pl.semaphore_wait(barrier, tiles - 1 + tasks - 1 + jnp.where(alone, 0, 1))

    scatter("a1", a1s, a1r)
    a2[me_j] = received("a1", a1s[me_j], a1r).astype(BF16)
    gather("a2", a2)
    wait(a2, tiles - 1, recv_sem, "a2")

    def project(blocks):
        basis = jnp.concatenate([blocks[j] for j in range(tiles)], axis=1)
        gram = dot(basis, basis, NT)
        product = jnp.zeros((RANK, width), F32)
        for n in range(CHUNKS):
            product += dot(basis[:, n * chunk : (n + 1) * chunk], dv[n * chunk : (n + 1) * chunk, :])
        factor = cholesky(lane_columns(gram))
        return jnp.concatenate(forward_solve(factor, to_tiles(product)), axis=1)

    power = project(a2)
    gps[...] = pack(dot_high(power, power, NT))
    to_each("gp", gps, gpr)

    parts = jnp.concatenate(three(power), axis=0)
    for n in range(CHUNKS):
        part = dot(parts, dv[n * chunk : (n + 1) * chunk, :], NT)
        high, low = split(part[:RANK] + (part[RANK : 2 * RANK] + part[2 * RANK :]))
        for m in range(chunk // LANES):
            c1s[n * (chunk // LANES) + m] = high[:, m * LANES : (m + 1) * LANES]
            c1xs[n * (chunk // LANES) + m] = low[:, m * LANES : (m + 1) * LANES]
    scatter("c1", c1s, c1r)
    scatter("c1x", c1xs, c1xr)

    power_factor = cholesky(lane_columns(unpack(received("gp", gps[...], gpr))))
    high = received("c1", c1s[me_j], c1r)
    c2[me_j] = forward_solve(power_factor, [high])[0].astype(BF16)
    gather("c2", c2)

    low = received("c1x", c1xs[me_j], c1xr)
    (left_slice,) = forward_solve(power_factor, [high + low])
    sl[...] = left_slice
    t1[me_t] = left_slice
    gls[...] = pack(dot_high(left_slice, left_slice, NT))
    to_task("t1", t1)
    to_each("gl", gls, glr)

    @pl.when(jnp.logical_not(alone))
    def _():
        send(sl, la.at[partner_j], "pm", partner_t, partner_j)

    @pl.when(alone)
    def _():
        la[me_j] = sl[...]

    wait(c2, tiles - 1, recv_sem, "c2")
    right = project(c2)
    high, low = split(right)
    eh[me_t] = high
    to_task("e", eh)
    grs[...] = pack(dot_high(right, right, NT))
    to_each("gr", grs, grr)
    el[me_t] = low
    to_task("el", el)

    dl[me_t] = received("gl", gls[...], glr)
    to_task_direct("dl", dl)
    pass_on("t1", t1)
    wait(t1, RING_Y, recv_sem, "t1c")
    stacked = split(jnp.concatenate([t1[t] for t in range(tasks)], axis=0))
    store_pieces(wls, fold(dot_split(stacked, stacked, NT)))
    scatter("rl", wls, wlr)

    @pl.when(jnp.logical_not(alone))
    def _():
        wait(la, 1, recv_sem, "pm")

    gather("la", la)

    pass_on("e", eh)
    wait(eh, RING_Y, recv_sem, "ec")
    stacked = jnp.concatenate([eh[t] for t in range(tasks)], axis=0)
    store_pieces(wrs, fold(dot(stacked, stacked, NT)))
    scatter("rr", wrs, wrr)

    dr[me_t] = received("gr", grs[...], grr)
    to_task_direct("dr", dr)
    pass_on("el", el)
    wlg[me_j] = received("rl", wls[me_j], wlr)
    gather("al", wlg)
    wrg[me_j] = received("rr", wrs[me_j], wrr)
    gather("ar", wrg)

    size = tasks * RANK
    eye = (rows_of((size, size)) == lanes_of((size, size))).astype(F32)
    wait(dl, tasks - 1, recv_sem, "dl")
    wait(dr, tasks - 1, recv_sem, "dr")
    left_blocks, right_blocks = side_by_side(dl), side_by_side(dr)
    left_inverse, right_inverse = block_factors((left_blocks, right_blocks))
    left_blocks, right_blocks = block_diagonal(left_blocks), block_diagonal(right_blocks)
    left_inverse, right_inverse = split(left_inverse), split(right_inverse)
    core_turned = dot_split(right_inverse, split(right_blocks))

    def orthonormal_gram(inverse, gram):
        return dot_split(split(dot_split(inverse, split(gram))), inverse, NT)

    wait(wlg, tiles - 1, recv_sem, "al")
    left_white = whitening(orthonormal_gram(left_inverse, unfold(pieces(wlg), left_blocks)), eye)
    wait(la, tiles - 1, recv_sem, "la")
    left_rows = jnp.concatenate(
        [
            jnp.concatenate([la[t * per_task + b] for b in range(per_task)], axis=1)
            for t in range(tasks)
        ],
        axis=0,
    )
    left = dot_split(left_inverse, split(left_rows))
    scaled = dot_split(split(core_turned), split(dot_split(split(left_white), split(left))))
    wait(el, RING_Y, recv_sem, "elc")
    right = (stacked, jnp.concatenate([el[t] for t in range(tasks)], axis=0))
    right = dot_split(right_inverse, right)

    wait(wrg, tiles - 1, recv_sem, "ar")
    right_white = whitening(orthonormal_gram(right_inverse, unfold(pieces(wrg), right_blocks)), eye)
    scaled = dot_split(split(right_white), split(scaled))
    out_ref[...] = dot_split(split(scaled), split(right), TN).astype(BF16)

    for name, ref, count in (
        ("a1", a1s, tiles - 1), ("a2", a2, tiles - 1), ("gp", gpr, tiles - 1), ("c1", c1s, tiles - 1),
        ("c1x", c1xs, tiles - 1), ("c2", c2, tiles - 1), ("gl", glr, tiles - 1), ("gr", grr, tiles - 1),
        ("t1y", t1, RING_Y - 1), ("t1c", t1, RING_Y), ("la", la, tiles - 1), ("ey", eh, RING_Y - 1),
        ("ec", eh, RING_Y), ("ely", el, RING_Y - 1), ("elc", el, RING_Y), ("dl", dl, tasks - 1),
        ("dr", dr, tasks - 1), ("rl", wls, tiles - 1), ("al", wlg, tiles - 1), ("rr", wrs, tiles - 1),
        ("ar", wrg, tiles - 1),
    ):
        wait(ref, count, send_sem, name)

    @pl.when(jnp.logical_not(alone))
    def _():
        wait(la, 1, send_sem, "pm")


def on_device(deltas, sketches):
    rows, width = deltas.shape[1:]
    tasks, tiles = RING_Y * CORES, RING_X * RING_Z
    block = (tiles, RANK, LANES)
    half = pltpu.VMEM(block, BF16)
    gram_in = pltpu.VMEM((tiles, 2, LANES), F32)
    gram_own = pltpu.VMEM((2, LANES), F32)
    gram_all = pltpu.VMEM((tasks, 2, LANES), F32)
    piece = pltpu.VMEM((tiles, 8, LANES), F32)
    return pl.pallas_call(
        kernel,
        out_shape=jax.ShapeDtypeStruct((rows // tasks, width), BF16),
        in_specs=[pl.BlockSpec(memory_space=pltpu.HBM)] * 2,
        out_specs=pl.BlockSpec(memory_space=pltpu.VMEM),
        scratch_shapes=[
            pltpu.VMEM((rows, width), BF16), pltpu.VMEM((RANK, width), BF16),
            half, half, half, gram_own, gram_in,
            half, half, half, half, half,
            gram_own, gram_in, gram_own, gram_in, gram_all, gram_all,
            pltpu.VMEM((RANK, LANES), F32), pltpu.VMEM((tasks, RANK, LANES), F32), pltpu.VMEM(block, F32),
            pltpu.VMEM((tasks, RANK, width), BF16), pltpu.VMEM((tasks, RANK, width), BF16),
            piece, piece, piece, piece, piece, piece,
            pltpu.SemaphoreType.DMA((CHUNKS + 1,)),
            pltpu.SemaphoreType.DMA((len(SEMS),)),
            pltpu.SemaphoreType.DMA((len(SEMS),)),
        ],
        compiler_params=pltpu.CompilerParams(
            collective_id=0, has_side_effects=True, vmem_limit_bytes=60 * 2**20
        ),
    )(deltas, jnp.swapaxes(sketches, 1, 2))


def solution(mesh):
    return jax.shard_map(
        on_device,
        mesh=mesh,
        in_specs=(P("task", None, "tile"), P("task", "tile", None)),
        out_specs=P("task", "tile"),
        check_vma=False,
    )
```

```python
import functools

import jax
import jax.numpy as jnp
from jax import lax
from jax.experimental import pallas as pl
from jax.experimental.pallas import tpu as pltpu
from jax.sharding import PartitionSpec as P

NEWTON = 5
RANK = 16
LANES = 128
RING_X, RING_Z = 4, 8
RING_Y, CORES = 8, 2
CHUNKS = 8
MESH = pl.DeviceIdType.MESH
HIGH = lax.Precision.HIGHEST
F32 = jnp.float32
BF16 = jnp.bfloat16

NN = (((1,), (0,)), ((), ()))
NT = (((1,), (1,)), ((), ()))
TN = (((0,), (0,)), ((), ()))

SEMS = ("a1", "a20", "a21", "a22", "a23", "gp", "c1", "c1x", "c20", "c21", "c22", "c23", "c2x", "gl", "t1y", "t1c",
        "lh", "ll", "ey", "ec", "ely", "elc", "gr", "dl", "dr", "rl", "al", "rr", "ar")
SEM = {name: index for index, name in enumerate(SEMS)}


def around(step, ring):
    return min(step, ring - step)


TILE_STEPS = sorted(
    ((a, b) for a in range(RING_X) for b in range(RING_Z) if (a, b) != (0, 0)),
    key=lambda step: -around(step[0], RING_X) - around(step[1], RING_Z),
)
X_STEPS = sorted(range(RING_X), key=lambda step: -around(step, RING_X))
Y_STEPS = sorted(range(1, RING_Y), key=lambda step: -around(step, RING_Y))
Z_STEPS = sorted(range(RING_Z), key=lambda step: -around(step, RING_Z))


def dot(a, b, dims=NN):
    return lax.dot_general(a, b, dims, preferred_element_type=F32)


def dot_high(a, b, dims=NN):
    return lax.dot_general(a, b, dims, precision=HIGH, preferred_element_type=F32)


def split(x):
    high = x.astype(BF16)
    return high, (x - high.astype(F32)).astype(BF16)


def dot_split(a, b, dims=NN):
    return dot(a[0], b[0], dims) + (dot(a[0], b[1], dims) + dot(a[1], b[0], dims))


def rsqrt(x):
    r = lax.rsqrt(x)
    return r * (1.5 - 0.5 * x * r * r)


def cholesky(columns):
    columns = list(columns)
    scales = []
    for k in range(RANK):
        scale = rsqrt(columns[k][k : k + 1, :])
        scales.append(scale)
        columns[k] = columns[k] * scale
        for i in range(k + 1, RANK):
            columns[i] = columns[i] - columns[k][i : i + 1, :] * columns[k]
    return columns, scales


def lane_columns(gram):
    return [jnp.broadcast_to(gram[:, i : i + 1], (RANK, LANES)) for i in range(RANK)]


def forward_solve(factor, tiles):
    columns, scales = factor
    row = rows_of((RANK, LANES))
    tiles = list(tiles)
    for k in range(RANK):
        below = jnp.where(row > k, columns[k], 0.0)
        at = row == k
        for n, tile in enumerate(tiles):
            solved = tile[k : k + 1, :] * scales[k]
            tiles[n] = jnp.where(at, jnp.broadcast_to(solved, tile.shape), tile - below * solved)
    return tiles


def to_tiles(matrix):
    return [matrix[:, n : n + LANES] for n in range(0, matrix.shape[1], LANES)]


def whitened(gram, matrix):
    size = gram.shape[0]
    eye = (rows_of((size, size)) == lanes_of((size, size))).astype(F32)
    squares = jnp.sum(gram * gram, keepdims=True)
    scale = jnp.sqrt(squares)
    product = gram / scale
    for step in range(NEWTON):
        halves = split(product)
        if step < NEWTON - 1:
            square = dot_split(halves, halves)
            following = dot_split(halves, split(2.25 * eye - 1.5 * product + 0.25 * square))
        matrix = dot_split(split(1.5 * eye - 0.5 * product), split(matrix))
        product = following
    return matrix / jnp.sqrt(scale)


def lanes_of(shape):
    return lax.broadcasted_iota(jnp.int32, shape, 1)


def rows_of(shape):
    return lax.broadcasted_iota(jnp.int32, shape, 0)


def repeat_lanes(wide):
    for shift in (RANK, 2 * RANK, 4 * RANK):
        wide = wide + pltpu.roll(wide, shift, 1)
    return wide


def pack(gram):
    shape = (RANK, LANES)
    wide = repeat_lanes(jnp.concatenate([gram, jnp.zeros((RANK, LANES - RANK), F32)], axis=1))
    wide = jnp.where(lanes_of(shape) // RANK == rows_of(shape) % 8, wide, 0.0)
    return jnp.concatenate(
        [jnp.sum(wide[:8], axis=0, keepdims=True), jnp.sum(wide[8:], axis=0, keepdims=True)], axis=0
    )


def unpack(packed):
    shape = (RANK, LANES)
    wide = jnp.where(rows_of(shape) < 8, packed[0:1, :], packed[1:2, :])
    return repeat_lanes(jnp.where(lanes_of(shape) // RANK == rows_of(shape) % 8, wide, 0.0))


def side_by_side(packed):
    shape = (RANK, LANES)
    halves = []
    for h in range(2):
        half = jnp.zeros(shape, F32)
        for b in range(8):
            half = jnp.where(lanes_of(shape) // RANK == b, unpack(packed[8 * h + b]), half)
        halves.append(half)
    return jnp.concatenate(halves, axis=1)


def block_diagonal(blocks):
    tasks = blocks.shape[1] // RANK
    lane = lanes_of(blocks.shape)
    return jnp.concatenate([jnp.where(lane // RANK == b, blocks, 0.0) for b in range(tasks)], axis=0)


def fold(gram):
    shape = (LANES, LANES)
    first = jnp.where(rows_of(shape) >= lanes_of(shape), gram[:LANES, :LANES], gram[LANES:, LANES:])
    return jnp.concatenate([first, gram[:LANES, LANES:]], axis=0)


def unfold(folded, blocks):
    shape = (LANES, LANES)
    first, cross = folded[:LANES], folded[LANES:]
    turned = first.T
    lower = rows_of(shape) >= lanes_of(shape)
    top = jnp.concatenate([jnp.where(lower, first, turned), cross], axis=1)
    bottom = jnp.concatenate([cross.T, jnp.where(lower, turned, first)], axis=1)
    gram = jnp.concatenate([top, bottom], axis=0)
    return jnp.where(rows_of(gram.shape) // RANK == lanes_of(gram.shape) // RANK, blocks, gram)


def three(x):
    first = x.astype(BF16)
    rest = x - first.astype(F32)
    second = rest.astype(BF16)
    return first, second, (rest - second.astype(F32)).astype(BF16)


def dot_ones(a, ones):
    first, second, third = three(a)
    return dot(first, ones) + (dot(second, ones) + dot(third, ones))


def block_factors(sides):
    size = sides[0].shape[1]
    tasks = size // RANK
    group = LANES // (2 * tasks)
    lane, sub = lanes_of((RANK, size)), rows_of((RANK, size))
    pick = lane % RANK == sub
    spread_row = rows_of((size, LANES)) // RANK
    spread_lane = lanes_of((size, LANES)) // group
    total = None
    for side, blocks in enumerate(sides):
        rows = [jnp.where(pick, jnp.broadcast_to(blocks[i : i + 1, :], (RANK, size)), 0.0) for i in range(RANK)]
        spread = (spread_lane == spread_row + side * tasks).astype(F32).astype(BF16)
        term = dot_ones(jnp.concatenate(rows, axis=0), spread)
        total = term if total is None else total + term
    columns, scales = cholesky([total[i * RANK : (i + 1) * RANK, :] for i in range(RANK)])
    row = rows_of((RANK, LANES))
    inverse = [(row == i).astype(F32) for i in range(RANK)]
    for k in range(RANK):
        inverse[k] = inverse[k] * scales[k]
        for i in range(k + 1, RANK):
            inverse[i] = inverse[i] - columns[k][i : i + 1, :] * inverse[k]
    stack = jnp.concatenate(inverse, axis=0)
    back_lane = rows_of((LANES, size))
    back_col = lanes_of((LANES, size)) // RANK
    factors = []
    for side in range(2):
        back = (back_lane == (back_col + side * tasks) * group).astype(F32).astype(BF16)
        wide = dot_ones(stack, back)
        rows = [
            jnp.sum(jnp.where(pick, wide[i * RANK : (i + 1) * RANK, :], 0.0), axis=0, keepdims=True) for i in range(RANK)
        ]
        factors.append(block_diagonal(jnp.concatenate(rows, axis=0)))
    return factors


def kernel(d_hbm, sk_hbm, out_ref, dv, skv, a1s, a1r, a2, gps, gpr, c1s, c1r, c1xs, c1xr, c2,
           c2x, gls, glr, grs, grr, dl, dr, t1, lh, ll, eh, el, wls, wlr, wlg, wrs, wrr, wrg,
           load_sem, send_sem, recv_sem):
    me_t, me_j = lax.axis_index("task"), lax.axis_index("tile")
    x, z = me_j // RING_Z, me_j % RING_Z
    y, core = me_t // CORES, me_t % CORES
    rows, width = dv.shape
    tiles, tasks = c2.shape[0], t1.shape[0]
    per_task = tiles // tasks
    chunk = rows // CHUNKS
    run = RING_Z * LANES

    xs = [((x + a) % RING_X) * RING_Z for a in range(RING_X)]
    zs = [(z + b) % RING_Z for b in range(RING_Z)]
    ys = [((y + c) % RING_Y) * CORES for c in range(RING_Y)]
    twin = y * CORES + (1 - core)

    barrier = pltpu.get_barrier_semaphore()

    def greet(t, j):
        pl.semaphore_signal(barrier, inc=1, device_id=(t, j), device_id_type=MESH)

    for a, b in TILE_STEPS:
        greet(me_t, xs[a] + zs[b])
    for c in Y_STEPS:
        greet(ys[c] + core, me_j)
        greet(ys[c] + (1 - core), me_j)
    greet(twin, me_j)

    sketch_load = pltpu.make_async_copy(sk_hbm.at[0], skv, load_sem.at[CHUNKS])
    sketch_load.start()
    loads = [
        pltpu.make_async_copy(
            d_hbm.at[0, pl.ds(n * chunk, chunk)], dv.at[pl.ds(n * chunk, chunk)], load_sem.at[n]
        )
        for n in range(CHUNKS)
    ]
    for load in loads:
        load.start()

    def send(src, dst, name, t, j):
        pltpu.make_async_remote_copy(
            src_ref=src, dst_ref=dst, send_sem=send_sem.at[SEM[name]], recv_sem=recv_sem.at[SEM[name]],
            device_id=(t, j), device_id_type=MESH,
        ).start()

    def wait(ref, count, sems, name):
        pltpu.make_async_copy(ref.at[pl.ds(0, count)], ref.at[pl.ds(0, count)], sems.at[SEM[name]]).wait()

    def scatter(name, src, dst):
        for a, b in TILE_STEPS:
            j = xs[a] + zs[b]
            send(src.at[j], dst.at[a * RING_Z + b], name, me_t, j)

    def to_each(name, src, dst):
        for a, b in TILE_STEPS:
            send(src, dst.at[a * RING_Z + b], name, me_t, xs[a] + zs[b])

    def gather(name, buf):
        for a, b in TILE_STEPS:
            send(buf.at[me_j], buf.at[me_j], name, me_t, xs[a] + zs[b])

    def gather_groups(name, buf):
        for a, b in TILE_STEPS:
            send(buf.at[me_j], buf.at[me_j], name + str(-a % RING_X), me_t, xs[a] + zs[b])

    def received(name, own, buf):
        wait(buf, tiles - 1, recv_sem, name)
        total = own.astype(F32)
        for k in range(1, tiles):
            total += buf[k].astype(F32)
        return total

    def to_task(name, buf):
        for c in Y_STEPS:
            send(buf.at[me_t], buf.at[me_t], name + "y", ys[c] + core, me_j)
        send(buf.at[me_t], buf.at[me_t], name + "c", twin, me_j)

    def pass_on(name, buf):
        wait(buf, RING_Y - 1, recv_sem, name + "y")
        for c in Y_STEPS:
            t = ys[c] + core
            send(buf.at[t], buf.at[t], name + "c", twin, me_j)

    def to_task_direct(name, src, dst):
        for t in [ys[c] + other for c in Y_STEPS for other in (core, 1 - core)] + [twin]:
            send(src(t), dst.at[me_t], name, t, me_j)

    def store_pieces(buf, matrix):
        for p in range(tiles):
            buf[p] = matrix[8 * p : 8 * p + 8, :]

    def pieces(buf):
        return jnp.concatenate([buf[p] for p in range(tiles)], axis=0)

    sketch_load.wait()
    sketch = skv[...]
    for n in range(CHUNKS):
        loads[n].wait()
        part = dot(sketch, dv[n * chunk : (n + 1) * chunk, :], NT).astype(BF16)
        for m in range(chunk // LANES):
            a1s[n * (chunk // LANES) + m] = part[:, m * LANES : (m + 1) * LANES]

    pl.semaphore_wait(barrier, tiles - 1 + tasks - 1)

    scatter("a1", a1s, a1r)
    a2[me_j] = received("a1", a1s[me_j], a1r).astype(BF16)
    gather_groups("a2", a2)

    def project(name, blocks):
        gram = jnp.zeros((RANK, RANK), F32)
        product = jnp.zeros((RANK, width), F32)
        for a in reversed(X_STEPS):
            wait(blocks, RING_Z - (a == 0), recv_sem, name + str(a))
            basis = jnp.concatenate([blocks[xs[a] + b] for b in range(RING_Z)], axis=1)
            product += dot(basis, dv[pl.ds(pl.multiple_of(xs[a] * LANES, run), run), :])
            gram += dot(basis, basis, NT)
        factor = cholesky(lane_columns(gram))
        return jnp.concatenate(forward_solve(factor, to_tiles(product)), axis=1)

    power = project("a2", a2)
    gps[...] = pack(dot_high(power, power, NT))

    parts = jnp.concatenate(three(power), axis=0)
    for n, a in enumerate(X_STEPS):
        part = dot(parts, dv[pl.ds(pl.multiple_of(xs[a] * LANES, run), run), :], NT)
        high, low = split(part[:RANK] + (part[RANK : 2 * RANK] + part[2 * RANK :]))
        for b in range(RING_Z):
            c1s[xs[a] + b] = high[:, b * LANES : (b + 1) * LANES]
            c1xs[xs[a] + b] = low[:, b * LANES : (b + 1) * LANES]
        for b in Z_STEPS:
            if (a, b) != (0, 0):
                send(c1s.at[xs[a] + zs[b]], c1r.at[a * RING_Z + b], "c1", me_t, xs[a] + zs[b])
        if n == 0:
            to_each("gp", gps, gpr)
    scatter("c1x", c1xs, c1xr)

    power_factor = cholesky(lane_columns(unpack(received("gp", gps[...], gpr))))
    high = received("c1", c1s[me_j], c1r)
    c2[me_j] = forward_solve(power_factor, [high])[0].astype(BF16)
    gather_groups("c2", c2)

    low = received("c1x", c1xs[me_j], c1xr)
    (left_slice,) = forward_solve(power_factor, [high + low])
    c2x[me_j] = (left_slice - c2[me_j].astype(F32)).astype(BF16)
    gather("c2x", c2x)
    t1[me_t] = left_slice
    gls[...] = pack(dot_high(left_slice, left_slice, NT))
    to_task("t1", t1)
    to_each("gl", gls, glr)

    right = project("c2", c2)
    high, low = split(right)
    eh[me_t] = high
    to_task("e", eh)
    grs[...] = pack(dot_high(right, right, NT))
    to_each("gr", grs, grr)
    el[me_t] = low
    to_task("el", el)

    dl[me_t] = received("gl", gls[...], glr)
    to_task_direct("dl", lambda t: dl.at[me_t], dl)
    pass_on("t1", t1)
    wait(t1, RING_Y, recv_sem, "t1c")
    stacked = split(jnp.concatenate([t1[t] for t in range(tasks)], axis=0))
    store_pieces(wls, fold(dot_split(stacked, stacked, NT)))
    scatter("rl", wls, wlr)

    pass_on("e", eh)
    wait(eh, RING_Y, recv_sem, "ec")
    stacked = jnp.concatenate([eh[t] for t in range(tasks)], axis=0)
    store_pieces(wrs, fold(dot(stacked, stacked, NT)))
    scatter("rr", wrs, wrr)

    wait(c2x, tiles - 1, recv_sem, "c2x")
    for name, src, dst in (("lh", c2, lh), ("ll", c2x, ll)):
        to_task_direct(name, lambda t: src.at[pl.ds(t * per_task, per_task)], dst)
        dst[me_t] = src[pl.ds(me_t * per_task, per_task)]

    dr[me_t] = received("gr", grs[...], grr)
    to_task_direct("dr", lambda t: dr.at[me_t], dr)
    pass_on("el", el)
    wlg[me_j] = received("rl", wls[me_j], wlr)
    gather("al", wlg)
    wrg[me_j] = received("rr", wrs[me_j], wrr)
    gather("ar", wrg)

    wait(dl, tasks - 1, recv_sem, "dl")
    wait(dr, tasks - 1, recv_sem, "dr")
    left_blocks, right_blocks = side_by_side(dl), side_by_side(dr)
    left_inverse, right_inverse = block_factors((left_blocks, right_blocks))
    left_blocks, right_blocks = block_diagonal(left_blocks), block_diagonal(right_blocks)
    left_inverse, right_inverse = split(left_inverse), split(right_inverse)
    core_turned = dot_split(right_inverse, split(right_blocks))

    def orthonormal_gram(inverse, gram):
        return dot_split(split(dot_split(inverse, split(gram))), inverse, NT)

    def rows_of_bases(buf):
        return jnp.concatenate(
            [jnp.concatenate([buf[t, b] for b in range(per_task)], axis=1) for t in range(tasks)], axis=0
        )

    wait(lh, tasks - 1, recv_sem, "lh")
    wait(ll, tasks - 1, recv_sem, "ll")
    left = dot_split(left_inverse, (rows_of_bases(lh), rows_of_bases(ll)))
    wait(wlg, tiles - 1, recv_sem, "al")
    left_gram = orthonormal_gram(left_inverse, unfold(pieces(wlg), left_blocks))
    scaled = dot_split(split(core_turned), split(whitened(left_gram, left)))
    wait(el, RING_Y, recv_sem, "elc")
    right = (stacked, jnp.concatenate([el[t] for t in range(tasks)], axis=0))
    right = dot_split(right_inverse, right)

    wait(wrg, tiles - 1, recv_sem, "ar")
    right_gram = orthonormal_gram(right_inverse, unfold(pieces(wrg), right_blocks))
    scaled = whitened(right_gram, scaled)
    out_ref[...] = dot_split(split(scaled), split(right), TN).astype(BF16)

    for name, ref, count in (
        ("a1", a1s, tiles - 1), ("gp", gpr, tiles - 1), ("c1", c1s, tiles - 1), ("c1x", c1xs, tiles - 1),
        ("c2x", c2x, tiles - 1), ("gl", glr, tiles - 1), ("gr", grr, tiles - 1),
        ("t1y", t1, RING_Y - 1), ("t1c", t1, RING_Y), ("lh", lh, tasks - 1), ("ll", ll, tasks - 1),
        ("ey", eh, RING_Y - 1), ("ec", eh, RING_Y), ("ely", el, RING_Y - 1), ("elc", el, RING_Y),
        ("dl", dl, tasks - 1), ("dr", dr, tasks - 1), ("rl", wls, tiles - 1), ("al", wlg, tiles - 1),
        ("rr", wrs, tiles - 1), ("ar", wrg, tiles - 1),
    ):
        wait(ref, count, send_sem, name)
    for a in range(RING_X):
        wait(a2, RING_Z - (a == 0), send_sem, "a2" + str(a))
        wait(c2, RING_Z - (a == 0), send_sem, "c2" + str(a))


def on_device(deltas, sketches):
    rows, width = deltas.shape[1:]
    tasks, tiles = RING_Y * CORES, RING_X * RING_Z
    block = (tiles, RANK, LANES)
    half = pltpu.VMEM(block, BF16)
    gram_in = pltpu.VMEM((tiles, 2, LANES), F32)
    gram_own = pltpu.VMEM((2, LANES), F32)
    gram_all = pltpu.VMEM((tasks, 2, LANES), F32)
    rows_all = pltpu.VMEM((tasks, tiles // tasks, RANK, LANES), BF16)
    piece = pltpu.VMEM((tiles, 8, LANES), F32)
    return pl.pallas_call(
        kernel,
        out_shape=jax.ShapeDtypeStruct((rows // tasks, width), BF16),
        in_specs=[pl.BlockSpec(memory_space=pltpu.HBM)] * 2,
        out_specs=pl.BlockSpec(memory_space=pltpu.VMEM),
        scratch_shapes=[
            pltpu.VMEM((rows, width), BF16), pltpu.VMEM((RANK, width), BF16),
            half, half, half, gram_own, gram_in,
            half, half, half, half, half,
            half, gram_own, gram_in, gram_own, gram_in, gram_all, gram_all,
            pltpu.VMEM((tasks, RANK, LANES), F32), rows_all, rows_all,
            pltpu.VMEM((tasks, RANK, width), BF16), pltpu.VMEM((tasks, RANK, width), BF16),
            piece, piece, piece, piece, piece, piece,
            pltpu.SemaphoreType.DMA((CHUNKS + 1,)),
            pltpu.SemaphoreType.DMA((len(SEMS),)),
            pltpu.SemaphoreType.DMA((len(SEMS),)),
        ],
        compiler_params=pltpu.CompilerParams(
            collective_id=0, has_side_effects=True, vmem_limit_bytes=52 * 2**20
        ),
    )(deltas, jnp.swapaxes(sketches, 1, 2))


def solution(mesh):
    return jax.shard_map(
        on_device,
        mesh=mesh,
        in_specs=(P("task", None, "tile"), P("task", "tile", None)),
        out_specs=P("task", "tile"),
        check_vma=False,
    )
```

```python
import functools

import jax
import jax.numpy as jnp
from jax import lax
from jax.experimental import pallas as pl
from jax.experimental.pallas import tpu as pltpu
from jax.sharding import PartitionSpec as P

NEWTON = 5
RANK = 16
LANES = 128
RING_X, RING_Z = 4, 8
RING_Y, CORES = 8, 2
CHUNKS = 8
MESH = pl.DeviceIdType.MESH
HIGH = lax.Precision.HIGHEST
F32 = jnp.float32
BF16 = jnp.bfloat16

NN = (((1,), (0,)), ((), ()))
NT = (((1,), (1,)), ((), ()))
TN = (((0,), (0,)), ((), ()))

SEMS = ("a1", "a20", "a21", "a22", "a23", "gp", "c1", "c1x", "c20", "c21", "c22", "c23", "c2x", "gl", "t1y", "t1c",
        "lh", "ll", "ey", "ec", "ely", "elc", "gr", "dl", "dr", "rl", "al", "rr", "ar")
SEM = {name: index for index, name in enumerate(SEMS)}


def around(step, ring):
    return min(step, ring - step)


TILE_STEPS = sorted(
    ((a, b) for a in range(RING_X) for b in range(RING_Z) if (a, b) != (0, 0)),
    key=lambda step: -around(step[0], RING_X) - around(step[1], RING_Z),
)
X_STEPS = sorted(range(RING_X), key=lambda step: -around(step, RING_X))
Y_STEPS = sorted(range(1, RING_Y), key=lambda step: -around(step, RING_Y))
Z_STEPS = sorted(range(RING_Z), key=lambda step: -around(step, RING_Z))


def dot(a, b, dims=NN):
    return lax.dot_general(a, b, dims, preferred_element_type=F32)


def dot_high(a, b, dims=NN):
    return lax.dot_general(a, b, dims, precision=HIGH, preferred_element_type=F32)


def split(x):
    high = x.astype(BF16)
    return high, (x - high.astype(F32)).astype(BF16)


def dot_split(a, b, dims=NN):
    return dot(a[0], b[0], dims) + (dot(a[0], b[1], dims) + dot(a[1], b[0], dims))


def rsqrt(x):
    r = lax.rsqrt(x)
    return r * (1.5 - 0.5 * x * r * r)


def cholesky(columns):
    columns = list(columns)
    scales = []
    for k in range(RANK):
        scale = rsqrt(columns[k][k : k + 1, :])
        scales.append(scale)
        columns[k] = columns[k] * scale
        for i in range(k + 1, RANK):
            columns[i] = columns[i] - columns[k][i : i + 1, :] * columns[k]
    return columns, scales


def lane_columns(gram):
    return [jnp.broadcast_to(gram[:, i : i + 1], (RANK, LANES)) for i in range(RANK)]


def forward_solve(factor, tiles):
    columns, scales = factor
    row = rows_of((RANK, LANES))
    tiles = list(tiles)
    for k in range(RANK):
        below = jnp.where(row > k, columns[k], 0.0)
        at = row == k
        for n, tile in enumerate(tiles):
            solved = tile[k : k + 1, :] * scales[k]
            tiles[n] = jnp.where(at, jnp.broadcast_to(solved, tile.shape), tile - below * solved)
    return tiles


def to_tiles(matrix):
    return [matrix[:, n : n + LANES] for n in range(0, matrix.shape[1], LANES)]


def whitened(gram, matrix):
    size = gram.shape[0]
    eye = (rows_of((size, size)) == lanes_of((size, size))).astype(F32)
    squares = jnp.sum(gram * gram, keepdims=True)
    scale = jnp.sqrt(squares)
    product = gram / scale
    for step in range(NEWTON):
        halves = split(product)
        if step < NEWTON - 1:
            square = dot_split(halves, halves)
            following = dot_split(halves, split(2.25 * eye - 1.5 * product + 0.25 * square))
        matrix = dot_split(split(1.5 * eye - 0.5 * product), split(matrix))
        product = following
    return matrix / jnp.sqrt(scale)


def lanes_of(shape):
    return lax.broadcasted_iota(jnp.int32, shape, 1)


def rows_of(shape):
    return lax.broadcasted_iota(jnp.int32, shape, 0)


def repeat_lanes(wide):
    for shift in (RANK, 2 * RANK, 4 * RANK):
        wide = wide + pltpu.roll(wide, shift, 1)
    return wide


def pack(gram):
    shape = (RANK, LANES)
    wide = repeat_lanes(jnp.concatenate([gram, jnp.zeros((RANK, LANES - RANK), F32)], axis=1))
    wide = jnp.where(lanes_of(shape) // RANK == rows_of(shape) % 8, wide, 0.0)
    return jnp.concatenate(
        [jnp.sum(wide[:8], axis=0, keepdims=True), jnp.sum(wide[8:], axis=0, keepdims=True)], axis=0
    )


def unpack(packed):
    shape = (RANK, LANES)
    wide = jnp.where(rows_of(shape) < 8, packed[0:1, :], packed[1:2, :])
    return repeat_lanes(jnp.where(lanes_of(shape) // RANK == rows_of(shape) % 8, wide, 0.0))


def side_by_side(packed):
    shape = (RANK, LANES)
    halves = []
    for h in range(2):
        half = jnp.zeros(shape, F32)
        for b in range(8):
            half = jnp.where(lanes_of(shape) // RANK == b, unpack(packed[8 * h + b]), half)
        halves.append(half)
    return jnp.concatenate(halves, axis=1)


def block_diagonal(blocks):
    tasks = blocks.shape[1] // RANK
    lane = lanes_of(blocks.shape)
    return jnp.concatenate([jnp.where(lane // RANK == b, blocks, 0.0) for b in range(tasks)], axis=0)


def fold(gram):
    shape = (LANES, LANES)
    first = jnp.where(rows_of(shape) >= lanes_of(shape), gram[:LANES, :LANES], gram[LANES:, LANES:])
    return jnp.concatenate([first, gram[:LANES, LANES:]], axis=0)


def unfold(folded, blocks):
    shape = (LANES, LANES)
    first, cross = folded[:LANES], folded[LANES:]
    turned = first.T
    lower = rows_of(shape) >= lanes_of(shape)
    top = jnp.concatenate([jnp.where(lower, first, turned), cross], axis=1)
    bottom = jnp.concatenate([cross.T, jnp.where(lower, turned, first)], axis=1)
    gram = jnp.concatenate([top, bottom], axis=0)
    return jnp.where(rows_of(gram.shape) // RANK == lanes_of(gram.shape) // RANK, blocks, gram)


def three(x):
    first = x.astype(BF16)
    rest = x - first.astype(F32)
    second = rest.astype(BF16)
    return first, second, (rest - second.astype(F32)).astype(BF16)


def dot_ones(a, ones):
    first, second, third = three(a)
    return dot(first, ones) + (dot(second, ones) + dot(third, ones))


def block_factors(sides):
    size = sides[0].shape[1]
    tasks = size // RANK
    group = LANES // (2 * tasks)
    lane, sub = lanes_of((RANK, size)), rows_of((RANK, size))
    pick = lane % RANK == sub
    spread_row = rows_of((size, LANES)) // RANK
    spread_lane = lanes_of((size, LANES)) // group
    total = None
    for side, blocks in enumerate(sides):
        rows = [jnp.where(pick, jnp.broadcast_to(blocks[i : i + 1, :], (RANK, size)), 0.0) for i in range(RANK)]
        spread = (spread_lane == spread_row + side * tasks).astype(F32).astype(BF16)
        term = dot_ones(jnp.concatenate(rows, axis=0), spread)
        total = term if total is None else total + term
    columns, scales = cholesky([total[i * RANK : (i + 1) * RANK, :] for i in range(RANK)])
    row = rows_of((RANK, LANES))
    inverse = [(row == i).astype(F32) for i in range(RANK)]
    for k in range(RANK):
        inverse[k] = inverse[k] * scales[k]
        for i in range(k + 1, RANK):
            inverse[i] = inverse[i] - columns[k][i : i + 1, :] * inverse[k]
    stack = jnp.concatenate(inverse, axis=0)
    back_lane = rows_of((LANES, size))
    back_col = lanes_of((LANES, size)) // RANK
    factors = []
    for side in range(2):
        back = (back_lane == (back_col + side * tasks) * group).astype(F32).astype(BF16)
        wide = dot_ones(stack, back)
        rows = [
            jnp.sum(jnp.where(pick, wide[i * RANK : (i + 1) * RANK, :], 0.0), axis=0, keepdims=True) for i in range(RANK)
        ]
        factors.append(block_diagonal(jnp.concatenate(rows, axis=0)))
    return factors


def kernel(d_hbm, sk_hbm, out_ref, dv, skv, a1s, a1r, a2, gps, gpr, c1s, c1r, c1xs, c1xr, c2,
           c2x, gls, glr, grs, grr, dl, dr, t1, lh, ll, eh, el, wls, wlr, wlg, wrs, wrr, wrg,
           load_sem, send_sem, recv_sem):
    me_t, me_j = lax.axis_index("task"), lax.axis_index("tile")
    x, z = me_j // RING_Z, me_j % RING_Z
    y, core = me_t // CORES, me_t % CORES
    rows, width = dv.shape
    tiles, tasks = c2.shape[0], t1.shape[0]
    per_task = tiles // tasks
    chunk = rows // CHUNKS
    run = RING_Z * LANES

    xs = [((x + a) % RING_X) * RING_Z for a in range(RING_X)]
    zs = [(z + b) % RING_Z for b in range(RING_Z)]
    ys = [((y + c) % RING_Y) * CORES for c in range(RING_Y)]
    twin = y * CORES + (1 - core)

    barrier = pltpu.get_barrier_semaphore()

    def greet(t, j):
        pl.semaphore_signal(barrier, inc=1, device_id=(t, j), device_id_type=MESH)

    for a, b in TILE_STEPS:
        greet(me_t, xs[a] + zs[b])
    for c in Y_STEPS:
        greet(ys[c] + core, me_j)
        greet(ys[c] + (1 - core), me_j)
    greet(twin, me_j)

    sketch_load = pltpu.make_async_copy(sk_hbm.at[0], skv, load_sem.at[CHUNKS])
    sketch_load.start()
    loads = [
        pltpu.make_async_copy(
            d_hbm.at[0, pl.ds(n * chunk, chunk)], dv.at[pl.ds(n * chunk, chunk)], load_sem.at[n]
        )
        for n in range(CHUNKS)
    ]
    for load in loads:
        load.start()

    def send(src, dst, name, t, j):
        pltpu.make_async_remote_copy(
            src_ref=src, dst_ref=dst, send_sem=send_sem.at[SEM[name]], recv_sem=recv_sem.at[SEM[name]],
            device_id=(t, j), device_id_type=MESH,
        ).start()

    def wait(ref, count, sems, name):
        pltpu.make_async_copy(ref.at[pl.ds(0, count)], ref.at[pl.ds(0, count)], sems.at[SEM[name]]).wait()

    def scatter(name, src, dst):
        for a, b in TILE_STEPS:
            j = xs[a] + zs[b]
            send(src.at[j], dst.at[a * RING_Z + b], name, me_t, j)

    def to_each(name, src, dst):
        for a, b in TILE_STEPS:
            send(src, dst.at[a * RING_Z + b], name, me_t, xs[a] + zs[b])

    def gather(name, buf):
        for a, b in TILE_STEPS:
            send(buf.at[me_j], buf.at[me_j], name, me_t, xs[a] + zs[b])

    def gather_groups(name, buf):
        for a, b in TILE_STEPS:
            send(buf.at[me_j], buf.at[me_j], name + str(-a % RING_X), me_t, xs[a] + zs[b])

    def received(name, own, buf):
        wait(buf, tiles - 1, recv_sem, name)
        total = own.astype(F32)
        for k in range(1, tiles):
            total += buf[k].astype(F32)
        return total

    def to_task(name, buf):
        for c in Y_STEPS:
            send(buf.at[me_t], buf.at[me_t], name + "y", ys[c] + core, me_j)
        send(buf.at[me_t], buf.at[me_t], name + "c", twin, me_j)

    def pass_on(name, buf):
        wait(buf, RING_Y - 1, recv_sem, name + "y")
        for c in Y_STEPS:
            t = ys[c] + core
            send(buf.at[t], buf.at[t], name + "c", twin, me_j)

    def to_task_direct(name, src, dst):
        for t in [ys[c] + other for c in Y_STEPS for other in (core, 1 - core)] + [twin]:
            send(src(t), dst.at[me_t], name, t, me_j)

    def store_pieces(buf, matrix):
        for p in range(tiles):
            buf[p] = matrix[8 * p : 8 * p + 8, :]

    def pieces(buf):
        return jnp.concatenate([buf[p] for p in range(tiles)], axis=0)

    sketch_load.wait()
    sketch = skv[...]
    for n in range(CHUNKS):
        loads[n].wait()
        part = dot(sketch, dv[n * chunk : (n + 1) * chunk, :], NT).astype(BF16)
        for m in range(chunk // LANES):
            a1s[n * (chunk // LANES) + m] = part[:, m * LANES : (m + 1) * LANES]

    pl.semaphore_wait(barrier, tiles - 1 + tasks - 1)

    scatter("a1", a1s, a1r)
    a2[me_j] = received("a1", a1s[me_j], a1r).astype(BF16)
    gather_groups("a2", a2)

    def project(name, blocks):
        gram = jnp.zeros((RANK, RANK), F32)
        product = jnp.zeros((RANK, width), F32)
        for a in reversed(X_STEPS):
            wait(blocks, RING_Z - (a == 0), recv_sem, name + str(a))
            basis = jnp.concatenate([blocks[xs[a] + b] for b in range(RING_Z)], axis=1)
            product += dot(basis, dv[pl.ds(pl.multiple_of(xs[a] * LANES, run), run), :])
            gram += dot(basis, basis, NT)
        factor = cholesky(lane_columns(gram))
        return jnp.concatenate(forward_solve(factor, to_tiles(product)), axis=1)

    power = project("a2", a2)
    gps[...] = pack(dot_high(power, power, NT))

    parts = jnp.concatenate(three(power), axis=0)
    for n, a in enumerate(X_STEPS):
        part = dot(parts, dv[pl.ds(pl.multiple_of(xs[a] * LANES, run), run), :], NT)
        high, low = split(part[:RANK] + (part[RANK : 2 * RANK] + part[2 * RANK :]))
        for b in range(RING_Z):
            c1s[xs[a] + b] = high[:, b * LANES : (b + 1) * LANES]
            c1xs[xs[a] + b] = low[:, b * LANES : (b + 1) * LANES]
        for b in Z_STEPS:
            if (a, b) != (0, 0):
                send(c1s.at[xs[a] + zs[b]], c1r.at[a * RING_Z + b], "c1", me_t, xs[a] + zs[b])
        if n == 0:
            to_each("gp", gps, gpr)
    scatter("c1x", c1xs, c1xr)

    power_factor = cholesky(lane_columns(unpack(received("gp", gps[...], gpr))))
    high = received("c1", c1s[me_j], c1r)
    c2[me_j] = forward_solve(power_factor, [high])[0].astype(BF16)
    gather_groups("c2", c2)

    low = received("c1x", c1xs[me_j], c1xr)
    (left_slice,) = forward_solve(power_factor, [high + low])
    c2x[me_j] = (left_slice - c2[me_j].astype(F32)).astype(BF16)
    t1[me_t] = left_slice
    gls[...] = pack(dot_high(left_slice, left_slice, NT))
    to_task("t1", t1)

    right = project("c2", c2)
    high, low = split(right)
    eh[me_t] = high
    to_task("e", eh)
    grs[...] = pack(dot_high(right, right, NT))
    to_each("gr", grs, grr)
    gather("c2x", c2x)
    to_each("gl", gls, glr)
    el[me_t] = low
    to_task("el", el)

    pass_on("t1", t1)
    wait(t1, RING_Y, recv_sem, "t1c")
    stacked = split(jnp.concatenate([t1[t] for t in range(tasks)], axis=0))
    store_pieces(wls, fold(dot_split(stacked, stacked, NT)))
    scatter("rl", wls, wlr)

    pass_on("e", eh)
    wait(eh, RING_Y, recv_sem, "ec")
    stacked = jnp.concatenate([eh[t] for t in range(tasks)], axis=0)
    store_pieces(wrs, fold(dot(stacked, stacked, NT)))
    scatter("rr", wrs, wrr)

    def left_rows(name, src, dst):
        to_task_direct(name, lambda t: src.at[pl.ds(t * per_task, per_task)], dst)
        dst[me_t] = src[pl.ds(me_t * per_task, per_task)]

    left_rows("lh", c2, lh)
    dl[me_t] = received("gl", gls[...], glr)
    to_task_direct("dl", lambda t: dl.at[me_t], dl)
    dr[me_t] = received("gr", grs[...], grr)
    to_task_direct("dr", lambda t: dr.at[me_t], dr)
    wlg[me_j] = received("rl", wls[me_j], wlr)
    gather("al", wlg)
    wait(c2x, tiles - 1, recv_sem, "c2x")
    left_rows("ll", c2x, ll)
    pass_on("el", el)
    wrg[me_j] = received("rr", wrs[me_j], wrr)
    gather("ar", wrg)

    wait(dl, tasks - 1, recv_sem, "dl")
    wait(dr, tasks - 1, recv_sem, "dr")
    left_blocks, right_blocks = side_by_side(dl), side_by_side(dr)
    left_inverse, right_inverse = block_factors((left_blocks, right_blocks))
    left_blocks, right_blocks = block_diagonal(left_blocks), block_diagonal(right_blocks)
    left_inverse, right_inverse = split(left_inverse), split(right_inverse)
    core_turned = dot_split(right_inverse, split(right_blocks))

    def orthonormal_gram(inverse, gram):
        return dot_split(split(dot_split(inverse, split(gram))), inverse, NT)

    def rows_of_bases(buf):
        return jnp.concatenate(
            [jnp.concatenate([buf[t, b] for b in range(per_task)], axis=1) for t in range(tasks)], axis=0
        )

    wait(lh, tasks - 1, recv_sem, "lh")
    wait(ll, tasks - 1, recv_sem, "ll")
    left = dot_split(left_inverse, (rows_of_bases(lh), rows_of_bases(ll)))
    wait(wlg, tiles - 1, recv_sem, "al")
    left_gram = orthonormal_gram(left_inverse, unfold(pieces(wlg), left_blocks))
    scaled = dot_split(split(core_turned), split(whitened(left_gram, left)))
    wait(el, RING_Y, recv_sem, "elc")
    right = (stacked, jnp.concatenate([el[t] for t in range(tasks)], axis=0))
    right = dot_split(right_inverse, right)

    wait(wrg, tiles - 1, recv_sem, "ar")
    right_gram = orthonormal_gram(right_inverse, unfold(pieces(wrg), right_blocks))
    scaled = whitened(right_gram, scaled)
    out_ref[...] = dot_split(split(scaled), split(right), TN).astype(BF16)

    for name, ref, count in (
        ("a1", a1s, tiles - 1), ("gp", gpr, tiles - 1), ("c1", c1s, tiles - 1), ("c1x", c1xs, tiles - 1),
        ("c2x", c2x, tiles - 1), ("gl", glr, tiles - 1), ("gr", grr, tiles - 1),
        ("t1y", t1, RING_Y - 1), ("t1c", t1, RING_Y), ("lh", lh, tasks - 1), ("ll", ll, tasks - 1),
        ("ey", eh, RING_Y - 1), ("ec", eh, RING_Y), ("ely", el, RING_Y - 1), ("elc", el, RING_Y),
        ("dl", dl, tasks - 1), ("dr", dr, tasks - 1), ("rl", wls, tiles - 1), ("al", wlg, tiles - 1),
        ("rr", wrs, tiles - 1), ("ar", wrg, tiles - 1),
    ):
        wait(ref, count, send_sem, name)
    for a in range(RING_X):
        wait(a2, RING_Z - (a == 0), send_sem, "a2" + str(a))
        wait(c2, RING_Z - (a == 0), send_sem, "c2" + str(a))


def on_device(deltas, sketches):
    rows, width = deltas.shape[1:]
    tasks, tiles = RING_Y * CORES, RING_X * RING_Z
    block = (tiles, RANK, LANES)
    half = pltpu.VMEM(block, BF16)
    gram_in = pltpu.VMEM((tiles, 2, LANES), F32)
    gram_own = pltpu.VMEM((2, LANES), F32)
    gram_all = pltpu.VMEM((tasks, 2, LANES), F32)
    rows_all = pltpu.VMEM((tasks, tiles // tasks, RANK, LANES), BF16)
    piece = pltpu.VMEM((tiles, 8, LANES), F32)
    return pl.pallas_call(
        kernel,
        out_shape=jax.ShapeDtypeStruct((rows // tasks, width), BF16),
        in_specs=[pl.BlockSpec(memory_space=pltpu.HBM)] * 2,
        out_specs=pl.BlockSpec(memory_space=pltpu.VMEM),
        scratch_shapes=[
            pltpu.VMEM((rows, width), BF16), pltpu.VMEM((RANK, width), BF16),
            half, half, half, gram_own, gram_in,
            half, half, half, half, half,
            half, gram_own, gram_in, gram_own, gram_in, gram_all, gram_all,
            pltpu.VMEM((tasks, RANK, LANES), F32), rows_all, rows_all,
            pltpu.VMEM((tasks, RANK, width), BF16), pltpu.VMEM((tasks, RANK, width), BF16),
            piece, piece, piece, piece, piece, piece,
            pltpu.SemaphoreType.DMA((CHUNKS + 1,)),
            pltpu.SemaphoreType.DMA((len(SEMS),)),
            pltpu.SemaphoreType.DMA((len(SEMS),)),
        ],
        compiler_params=pltpu.CompilerParams(
            collective_id=0, has_side_effects=True, vmem_limit_bytes=52 * 2**20
        ),
    )(
        pltpu.with_memory_space_constraint(deltas, pltpu.HBM),
        pltpu.with_memory_space_constraint(jnp.swapaxes(sketches, 1, 2), pltpu.HBM),
    )


def solution(mesh):
    return jax.shard_map(
        on_device,
        mesh=mesh,
        in_specs=(P("task", None, "tile"), P("task", "tile", None)),
        out_specs=P("task", "tile"),
        check_vma=False,
    )
```

```python
import functools

import jax
import jax.numpy as jnp
from jax import lax
from jax.experimental import pallas as pl
from jax.experimental.pallas import tpu as pltpu
from jax.sharding import PartitionSpec as P

NEWTON = 5
RANK = 16
LANES = 128
RING_X, RING_Z = 4, 8
RING_Y, CORES = 8, 2
CHUNKS = 8
MESH = pl.DeviceIdType.MESH
HIGH = lax.Precision.HIGHEST
F32 = jnp.float32
BF16 = jnp.bfloat16

NN = (((1,), (0,)), ((), ()))
NT = (((1,), (1,)), ((), ()))
TN = (((0,), (0,)), ((), ()))

SEMS = ("a1", "a20", "a21", "a22", "a23", "gp", "c1", "c1x", "c20", "c21", "c22", "c23", "c2x", "gl", "t1y", "t1c",
        "lh", "ll", "en", "ey", "ec", "ely", "elc", "gr", "dl", "dr", "rl", "al", "rr", "ar")
SEM = {name: index for index, name in enumerate(SEMS)}


def around(step, ring):
    return min(step, ring - step)


TILE_STEPS = sorted(
    ((a, b) for a in range(RING_X) for b in range(RING_Z) if (a, b) != (0, 0)),
    key=lambda step: -around(step[0], RING_X) - around(step[1], RING_Z),
)
X_STEPS = sorted(range(RING_X), key=lambda step: -around(step, RING_X))
Y_STEPS = sorted(range(1, RING_Y), key=lambda step: -around(step, RING_Y))
Z_STEPS = sorted(range(RING_Z), key=lambda step: -around(step, RING_Z))


def dot(a, b, dims=NN):
    return lax.dot_general(a, b, dims, preferred_element_type=F32)


def dot_high(a, b, dims=NN):
    return lax.dot_general(a, b, dims, precision=HIGH, preferred_element_type=F32)


def split(x):
    high = x.astype(BF16)
    return high, (x - high.astype(F32)).astype(BF16)


def dot_split(a, b, dims=NN):
    return dot(a[0], b[0], dims) + (dot(a[0], b[1], dims) + dot(a[1], b[0], dims))


def rsqrt(x):
    r = lax.rsqrt(x)
    return r * (1.5 - 0.5 * x * r * r)


def cholesky(columns):
    columns = list(columns)
    scales = []
    for k in range(RANK):
        scale = rsqrt(columns[k][k : k + 1, :])
        scales.append(scale)
        columns[k] = columns[k] * scale
        for i in range(k + 1, RANK):
            columns[i] = columns[i] - columns[k][i : i + 1, :] * columns[k]
    return columns, scales


def lane_columns(gram):
    return [jnp.broadcast_to(gram[:, i : i + 1], (RANK, LANES)) for i in range(RANK)]


def forward_solve(factor, tiles):
    columns, scales = factor
    row = rows_of((RANK, LANES))
    tiles = list(tiles)
    for k in range(RANK):
        below = jnp.where(row > k, columns[k], 0.0)
        at = row == k
        for n, tile in enumerate(tiles):
            solved = tile[k : k + 1, :] * scales[k]
            tiles[n] = jnp.where(at, jnp.broadcast_to(solved, tile.shape), tile - below * solved)
    return tiles


def to_tiles(matrix):
    return [matrix[:, n : n + LANES] for n in range(0, matrix.shape[1], LANES)]


def whitened(gram, matrix):
    size = gram.shape[0]
    eye = (rows_of((size, size)) == lanes_of((size, size))).astype(F32)
    squares = jnp.sum(gram * gram, keepdims=True)
    scale = jnp.sqrt(squares)
    product = gram / scale
    for step in range(NEWTON):
        halves = split(product)
        if step < NEWTON - 1:
            square = dot_split(halves, halves)
            following = dot_split(halves, split(2.25 * eye - 1.5 * product + 0.25 * square))
        matrix = dot_split(split(1.5 * eye - 0.5 * product), split(matrix))
        product = following
    return matrix / jnp.sqrt(scale)


def lanes_of(shape):
    return lax.broadcasted_iota(jnp.int32, shape, 1)


def rows_of(shape):
    return lax.broadcasted_iota(jnp.int32, shape, 0)


def repeat_lanes(wide):
    for shift in (RANK, 2 * RANK, 4 * RANK):
        wide = wide + pltpu.roll(wide, shift, 1)
    return wide


def pack(gram):
    shape = (RANK, LANES)
    wide = repeat_lanes(jnp.concatenate([gram, jnp.zeros((RANK, LANES - RANK), F32)], axis=1))
    wide = jnp.where(lanes_of(shape) // RANK == rows_of(shape) % 8, wide, 0.0)
    return jnp.concatenate(
        [jnp.sum(wide[:8], axis=0, keepdims=True), jnp.sum(wide[8:], axis=0, keepdims=True)], axis=0
    )


def unpack(packed):
    shape = (RANK, LANES)
    wide = jnp.where(rows_of(shape) < 8, packed[0:1, :], packed[1:2, :])
    return repeat_lanes(jnp.where(lanes_of(shape) // RANK == rows_of(shape) % 8, wide, 0.0))


def side_by_side(packed):
    shape = (RANK, LANES)
    halves = []
    for h in range(2):
        half = jnp.zeros(shape, F32)
        for b in range(8):
            half = jnp.where(lanes_of(shape) // RANK == b, unpack(packed[8 * h + b]), half)
        halves.append(half)
    return jnp.concatenate(halves, axis=1)


def block_diagonal(blocks):
    tasks = blocks.shape[1] // RANK
    lane = lanes_of(blocks.shape)
    return jnp.concatenate([jnp.where(lane // RANK == b, blocks, 0.0) for b in range(tasks)], axis=0)


def fold(gram):
    shape = (LANES, LANES)
    first = jnp.where(rows_of(shape) >= lanes_of(shape), gram[:LANES, :LANES], gram[LANES:, LANES:])
    return jnp.concatenate([first, gram[:LANES, LANES:]], axis=0)


def unfold(folded, blocks):
    shape = (LANES, LANES)
    first, cross = folded[:LANES], folded[LANES:]
    turned = first.T
    lower = rows_of(shape) >= lanes_of(shape)
    top = jnp.concatenate([jnp.where(lower, first, turned), cross], axis=1)
    bottom = jnp.concatenate([cross.T, jnp.where(lower, turned, first)], axis=1)
    gram = jnp.concatenate([top, bottom], axis=0)
    return jnp.where(rows_of(gram.shape) // RANK == lanes_of(gram.shape) // RANK, blocks, gram)


def three(x):
    first = x.astype(BF16)
    rest = x - first.astype(F32)
    second = rest.astype(BF16)
    return first, second, (rest - second.astype(F32)).astype(BF16)


def dot_ones(a, ones):
    first, second, third = three(a)
    return dot(first, ones) + (dot(second, ones) + dot(third, ones))


def block_factors(sides):
    size = sides[0].shape[1]
    tasks = size // RANK
    group = LANES // (2 * tasks)
    lane, sub = lanes_of((RANK, size)), rows_of((RANK, size))
    pick = lane % RANK == sub
    spread_row = rows_of((size, LANES)) // RANK
    spread_lane = lanes_of((size, LANES)) // group
    total = None
    for side, blocks in enumerate(sides):
        rows = [jnp.where(pick, jnp.broadcast_to(blocks[i : i + 1, :], (RANK, size)), 0.0) for i in range(RANK)]
        spread = (spread_lane == spread_row + side * tasks).astype(F32).astype(BF16)
        term = dot_ones(jnp.concatenate(rows, axis=0), spread)
        total = term if total is None else total + term
    columns, scales = cholesky([total[i * RANK : (i + 1) * RANK, :] for i in range(RANK)])
    row = rows_of((RANK, LANES))
    inverse = [(row == i).astype(F32) for i in range(RANK)]
    for k in range(RANK):
        inverse[k] = inverse[k] * scales[k]
        for i in range(k + 1, RANK):
            inverse[i] = inverse[i] - columns[k][i : i + 1, :] * inverse[k]
    stack = jnp.concatenate(inverse, axis=0)
    back_lane = rows_of((LANES, size))
    back_col = lanes_of((LANES, size)) // RANK
    factors = []
    for side in range(2):
        back = (back_lane == (back_col + side * tasks) * group).astype(F32).astype(BF16)
        wide = dot_ones(stack, back)
        rows = [
            jnp.sum(jnp.where(pick, wide[i * RANK : (i + 1) * RANK, :], 0.0), axis=0, keepdims=True) for i in range(RANK)
        ]
        factors.append(block_diagonal(jnp.concatenate(rows, axis=0)))
    return factors


def kernel(d_hbm, sk_hbm, out_ref, dv, skv, a1s, a1r, a2, gps, gpr, c1s, c1r, c1xs, c1xr, c2,
           c2x, gls, glr, grs, grr, dl, dr, t1, lh, ll, eh, el, wls, wlr, wlg, wrs, wrr, wrg,
           load_sem, send_sem, recv_sem):
    me_t, me_j = lax.axis_index("task"), lax.axis_index("tile")
    x, z = me_j // RING_Z, me_j % RING_Z
    y, core = me_t // CORES, me_t % CORES
    rows, width = dv.shape
    tiles, tasks = c2.shape[0], t1.shape[0]
    per_task = tiles // tasks
    chunk = rows // CHUNKS
    run = RING_Z * LANES

    xs = [((x + a) % RING_X) * RING_Z for a in range(RING_X)]
    zs = [(z + b) % RING_Z for b in range(RING_Z)]
    ys = [((y + c) % RING_Y) * CORES for c in range(RING_Y)]
    twin = y * CORES + (1 - core)

    barrier = pltpu.get_barrier_semaphore()

    def greet(t, j):
        pl.semaphore_signal(barrier, inc=1, device_id=(t, j), device_id_type=MESH)

    for a, b in TILE_STEPS:
        greet(me_t, xs[a] + zs[b])
    for c in Y_STEPS:
        greet(ys[c] + core, me_j)
        greet(ys[c] + (1 - core), me_j)
    greet(twin, me_j)

    sketch_load = pltpu.make_async_copy(sk_hbm.at[0], skv, load_sem.at[CHUNKS])
    sketch_load.start()
    loads = [
        pltpu.make_async_copy(
            d_hbm.at[0, pl.ds(n * chunk, chunk)], dv.at[pl.ds(n * chunk, chunk)], load_sem.at[n]
        )
        for n in range(CHUNKS)
    ]
    for load in loads:
        load.start()

    def send(src, dst, name, t, j):
        pltpu.make_async_remote_copy(
            src_ref=src, dst_ref=dst, send_sem=send_sem.at[SEM[name]], recv_sem=recv_sem.at[SEM[name]],
            device_id=(t, j), device_id_type=MESH,
        ).start()

    def wait(ref, count, sems, name):
        pltpu.make_async_copy(ref.at[pl.ds(0, count)], ref.at[pl.ds(0, count)], sems.at[SEM[name]]).wait()

    def scatter(name, src, dst):
        for a, b in TILE_STEPS:
            j = xs[a] + zs[b]
            send(src.at[j], dst.at[a * RING_Z + b], name, me_t, j)

    def to_each(name, src, dst):
        for a, b in TILE_STEPS:
            send(src, dst.at[a * RING_Z + b], name, me_t, xs[a] + zs[b])

    def gather(name, buf):
        for a, b in TILE_STEPS:
            send(buf.at[me_j], buf.at[me_j], name, me_t, xs[a] + zs[b])

    def gather_groups(name, buf):
        for a, b in TILE_STEPS:
            send(buf.at[me_j], buf.at[me_j], name + str(-a % RING_X), me_t, xs[a] + zs[b])

    def received(name, own, buf):
        wait(buf, tiles - 1, recv_sem, name)
        total = own.astype(F32)
        for k in range(1, tiles):
            total += buf[k].astype(F32)
        return total

    def to_task(name, buf):
        for c in Y_STEPS:
            send(buf.at[me_t], buf.at[me_t], name + "y", ys[c] + core, me_j)
        send(buf.at[me_t], buf.at[me_t], name + "c", twin, me_j)

    def pass_on(name, buf):
        wait(buf, RING_Y - 1, recv_sem, name + "y")
        for c in Y_STEPS:
            t = ys[c] + core
            send(buf.at[t], buf.at[t], name + "c", twin, me_j)

    def to_task_direct(name, src, dst):
        for t in [ys[c] + other for c in Y_STEPS for other in (core, 1 - core)] + [twin]:
            send(src(t), dst.at[me_t], name, t, me_j)

    def store_pieces(buf, matrix):
        for p in range(tiles):
            buf[p] = matrix[8 * p : 8 * p + 8, :]

    def pieces(buf):
        return jnp.concatenate([buf[p] for p in range(tiles)], axis=0)

    sketch_load.wait()
    sketch = skv[...]
    for n in range(CHUNKS):
        loads[n].wait()
        part = dot(sketch, dv[n * chunk : (n + 1) * chunk, :], NT).astype(BF16)
        for m in range(chunk // LANES):
            a1s[n * (chunk // LANES) + m] = part[:, m * LANES : (m + 1) * LANES]

    pl.semaphore_wait(barrier, tiles - 1 + tasks - 1)

    scatter("a1", a1s, a1r)
    a2[me_j] = received("a1", a1s[me_j], a1r).astype(BF16)
    gather_groups("a2", a2)

    def project(name, blocks):
        gram = jnp.zeros((RANK, RANK), F32)
        product = jnp.zeros((RANK, width), F32)
        for a in reversed(X_STEPS):
            wait(blocks, RING_Z - (a == 0), recv_sem, name + str(a))
            basis = jnp.concatenate([blocks[xs[a] + b] for b in range(RING_Z)], axis=1)
            product += dot(basis, dv[pl.ds(pl.multiple_of(xs[a] * LANES, run), run), :])
            gram += dot(basis, basis, NT)
        factor = cholesky(lane_columns(gram))
        return jnp.concatenate(forward_solve(factor, to_tiles(product)), axis=1)

    power = project("a2", a2)
    gps[...] = pack(dot_high(power, power, NT))

    parts = jnp.concatenate(three(power), axis=0)
    for n, a in enumerate(X_STEPS):
        part = dot(parts, dv[pl.ds(pl.multiple_of(xs[a] * LANES, run), run), :], NT)
        high, low = split(part[:RANK] + (part[RANK : 2 * RANK] + part[2 * RANK :]))
        for b in range(RING_Z):
            c1s[xs[a] + b] = high[:, b * LANES : (b + 1) * LANES]
            c1xs[xs[a] + b] = low[:, b * LANES : (b + 1) * LANES]
        for b in Z_STEPS:
            if (a, b) != (0, 0):
                send(c1s.at[xs[a] + zs[b]], c1r.at[a * RING_Z + b], "c1", me_t, xs[a] + zs[b])
        if n == 0:
            to_each("gp", gps, gpr)
    scatter("c1x", c1xs, c1xr)

    power_factor = cholesky(lane_columns(unpack(received("gp", gps[...], gpr))))
    high = received("c1", c1s[me_j], c1r)
    c2[me_j] = forward_solve(power_factor, [high])[0].astype(BF16)
    gather_groups("c2", c2)

    low = received("c1x", c1xs[me_j], c1xr)
    (left_slice,) = forward_solve(power_factor, [high + low])
    c2x[me_j] = (left_slice - c2[me_j].astype(F32)).astype(BF16)
    t1[me_t] = left_slice
    gls[...] = pack(dot_high(left_slice, left_slice, NT))
    to_task("t1", t1)

    right = project("c2", c2)
    high, low = split(right)
    eh[me_t] = high
    for c in Y_STEPS:
        send(eh.at[me_t], eh.at[me_t], "ey" if around(c, RING_Y) > 2 else "en", ys[c] + core, me_j)
    send(eh.at[me_t], eh.at[me_t], "ec", twin, me_j)
    grs[...] = pack(dot_high(right, right, NT))
    to_each("gr", grs, grr)
    gather("c2x", c2x)
    to_each("gl", gls, glr)
    el[me_t] = low
    to_task("el", el)

    pass_on("t1", t1)
    wait(t1, RING_Y, recv_sem, "t1c")
    stacked = split(jnp.concatenate([t1[t] for t in range(tasks)], axis=0))
    store_pieces(wls, fold(dot_split(stacked, stacked, NT)))
    scatter("rl", wls, wlr)

    for name, near in (("en", True), ("ey", False)):
        group = [c for c in Y_STEPS if (around(c, RING_Y) <= 2) == near]
        wait(eh, len(group), recv_sem, name)
        for c in group:
            send(eh.at[ys[c] + core], eh.at[ys[c] + core], "ec", twin, me_j)
    wait(eh, RING_Y, recv_sem, "ec")
    stacked = jnp.concatenate([eh[t] for t in range(tasks)], axis=0)
    store_pieces(wrs, fold(dot(stacked, stacked, NT)))
    scatter("rr", wrs, wrr)

    def left_rows(name, src, dst):
        to_task_direct(name, lambda t: src.at[pl.ds(t * per_task, per_task)], dst)
        dst[me_t] = src[pl.ds(me_t * per_task, per_task)]

    dl[me_t] = received("gl", gls[...], glr)
    to_task_direct("dl", lambda t: dl.at[me_t], dl)
    dr[me_t] = received("gr", grs[...], grr)
    to_task_direct("dr", lambda t: dr.at[me_t], dr)
    wlg[me_j] = received("rl", wls[me_j], wlr)
    gather("al", wlg)
    left_rows("lh", c2, lh)
    wait(c2x, tiles - 1, recv_sem, "c2x")
    left_rows("ll", c2x, ll)
    pass_on("el", el)
    wrg[me_j] = received("rr", wrs[me_j], wrr)
    gather("ar", wrg)

    wait(dl, tasks - 1, recv_sem, "dl")
    wait(dr, tasks - 1, recv_sem, "dr")
    left_blocks, right_blocks = side_by_side(dl), side_by_side(dr)
    left_inverse, right_inverse = block_factors((left_blocks, right_blocks))
    left_blocks, right_blocks = block_diagonal(left_blocks), block_diagonal(right_blocks)
    left_inverse, right_inverse = split(left_inverse), split(right_inverse)
    core_turned = dot_split(right_inverse, split(right_blocks))

    def orthonormal_gram(inverse, gram):
        return dot_split(split(dot_split(inverse, split(gram))), inverse, NT)

    def rows_of_bases(buf):
        return jnp.concatenate(
            [jnp.concatenate([buf[t, b] for b in range(per_task)], axis=1) for t in range(tasks)], axis=0
        )

    wait(lh, tasks - 1, recv_sem, "lh")
    wait(ll, tasks - 1, recv_sem, "ll")
    left = dot_split(left_inverse, (rows_of_bases(lh), rows_of_bases(ll)))
    wait(wlg, tiles - 1, recv_sem, "al")
    left_gram = orthonormal_gram(left_inverse, unfold(pieces(wlg), left_blocks))
    scaled = dot_split(split(core_turned), split(whitened(left_gram, left)))
    wait(el, RING_Y, recv_sem, "elc")
    right = (stacked, jnp.concatenate([el[t] for t in range(tasks)], axis=0))
    right = dot_split(right_inverse, right)

    wait(wrg, tiles - 1, recv_sem, "ar")
    right_gram = orthonormal_gram(right_inverse, unfold(pieces(wrg), right_blocks))
    scaled = whitened(right_gram, scaled)
    out_ref[...] = dot_split(split(scaled), split(right), TN).astype(BF16)

    for name, ref, count in (
        ("a1", a1s, tiles - 1), ("gp", gpr, tiles - 1), ("c1", c1s, tiles - 1), ("c1x", c1xs, tiles - 1),
        ("c2x", c2x, tiles - 1), ("gl", glr, tiles - 1), ("gr", grr, tiles - 1),
        ("t1y", t1, RING_Y - 1), ("t1c", t1, RING_Y), ("lh", lh, tasks - 1), ("ll", ll, tasks - 1),
        ("en", eh, 4), ("ey", eh, RING_Y - 5), ("ec", eh, RING_Y), ("ely", el, RING_Y - 1), ("elc", el, RING_Y),
        ("dl", dl, tasks - 1), ("dr", dr, tasks - 1), ("rl", wls, tiles - 1), ("al", wlg, tiles - 1),
        ("rr", wrs, tiles - 1), ("ar", wrg, tiles - 1),
    ):
        wait(ref, count, send_sem, name)
    for a in range(RING_X):
        wait(a2, RING_Z - (a == 0), send_sem, "a2" + str(a))
        wait(c2, RING_Z - (a == 0), send_sem, "c2" + str(a))


def on_device(deltas, sketches):
    rows, width = deltas.shape[1:]
    tasks, tiles = RING_Y * CORES, RING_X * RING_Z
    block = (tiles, RANK, LANES)
    half = pltpu.VMEM(block, BF16)
    gram_in = pltpu.VMEM((tiles, 2, LANES), F32)
    gram_own = pltpu.VMEM((2, LANES), F32)
    gram_all = pltpu.VMEM((tasks, 2, LANES), F32)
    rows_all = pltpu.VMEM((tasks, tiles // tasks, RANK, LANES), BF16)
    piece = pltpu.VMEM((tiles, 8, LANES), F32)
    return pl.pallas_call(
        kernel,
        out_shape=jax.ShapeDtypeStruct((rows // tasks, width), BF16),
        in_specs=[pl.BlockSpec(memory_space=pltpu.HBM)] * 2,
        out_specs=pl.BlockSpec(memory_space=pltpu.VMEM),
        scratch_shapes=[
            pltpu.VMEM((rows, width), BF16), pltpu.VMEM((RANK, width), BF16),
            half, half, half, gram_own, gram_in,
            half, half, half, half, half,
            half, gram_own, gram_in, gram_own, gram_in, gram_all, gram_all,
            pltpu.VMEM((tasks, RANK, LANES), F32), rows_all, rows_all,
            pltpu.VMEM((tasks, RANK, width), BF16), pltpu.VMEM((tasks, RANK, width), BF16),
            piece, piece, piece, piece, piece, piece,
            pltpu.SemaphoreType.DMA((CHUNKS + 1,)),
            pltpu.SemaphoreType.DMA((len(SEMS),)),
            pltpu.SemaphoreType.DMA((len(SEMS),)),
        ],
        compiler_params=pltpu.CompilerParams(
            collective_id=0, has_side_effects=True, vmem_limit_bytes=52 * 2**20
        ),
    )(
        pltpu.with_memory_space_constraint(deltas, pltpu.HBM),
        pltpu.with_memory_space_constraint(jnp.swapaxes(sketches, 1, 2), pltpu.HBM),
    )


def solution(mesh):
    return jax.shard_map(
        on_device,
        mesh=mesh,
        in_specs=(P("task", None, "tile"), P("task", "tile", None)),
        out_specs=P("task", "tile"),
        check_vma=False,
    )
```
